256 devices in a mesh: seq: 32 (over y_hi, z, core), head: 8 (over y_lo, x).
Axes of the slice: x: 4, y: 4 (y_hi: 2, y_lo: 2; y = y_hi * 2 + y_lo), z: 8, core: 2. Of those that a mesh axis runs over, the one named last changes fastest.
Arguments:
- query_proj: bfloat16 [12288, 2048], P('seq', 'head'), may hold values from -100 to 100
- key_proj: bfloat16 [12288, 2048], P('seq', 'head'), may hold values from -4 to 4
- value_proj: bfloat16 [12288, 2048], P('seq', 'head'), may hold values from -6 to 6
- query_tangent: bfloat16 [12288, 2048], P('seq', 'head'), may hold values from -6 to 6
- key_tangent: bfloat16 [12288, 2048], P('seq', 'head'), may hold values from -6 to 6
- value_tangent: bfloat16 [12288, 2048], P('seq', 'head'), may hold values from -16 to 16
Outputs:
- attended: bfloat16 [12288, 2048], P('seq', 'head')
- tangent_unit: bfloat16 [12288, 2048], P('seq', 'head')
The draws below stay inside these ranges and needn't reach their ends.
All inputs are finite; a program needn't handle non-finite values.
Results may differ from the reference program's by a relative error of at most 0.0095.
Values may be sent and summed in bfloat16 or wider, within the bound.
No kernel may reach another device: no remote copies, remote signals or barrier semaphores. Data moves between devices by JAX's collectives and lax.ppermute only.
A program may use at most 128 MiB of HBM per device.

```python
import math
import jax
import jax.numpy as jnp
from jax import lax

HEADS = 16
DH = 128
TOKENS = 12288


def base_keys(key):
    return jnp.clip(jax.random.normal(key, (TOKENS, HEADS * DH), jnp.float32), -4.0, 4.0)


def draw_key_proj(key, part):
    shared = base_keys(key)
    return shared.astype(jnp.bfloat16)


def draw_query_proj(key, part):
    key = jax.random.fold_in(key, 5)
    fresh = jnp.clip(jax.random.normal(key, (TOKENS, HEADS * DH), jnp.float32), -4.0, 4.0)
    return fresh.astype(jnp.bfloat16)


def draw_value_tangent(key, part):
    key = jax.random.fold_in(key, 7)
    position = (jnp.arange(HEADS * DH) // DH).astype(jnp.float32) / (HEADS - 1)
    ramp = 1.0 + 2.0 * position
    fresh = jnp.clip(jax.random.normal(key, (TOKENS, HEADS * DH), jnp.float32), -4.0, 4.0)
    return (fresh * ramp[None, :]).astype(jnp.bfloat16)


def level_of(stream_key, extent, shards, least, largest):
    loudness = 1.0
    for axis_at, shards_of in shards:
        steps = jax.random.uniform(jax.random.fold_in(jax.random.fold_in(stream_key, 6), axis_at), (shards_of,), jnp.float32, least / len(shards), largest / len(shards))
        loudness = loudness * jnp.repeat(jnp.exp(steps), extent[axis_at] // shards_of).reshape((-1,) + (1,) * (len(extent) - 1 - axis_at))
    return loudness


def bell_draw(own_key, dims, width, bound, pieces=(), held_as=jnp.bfloat16):
    loudness = level_of(own_key, dims, pieces, -0.22, 0.18) if pieces else 1.0
    result = jax.random.normal(own_key, dims, jnp.float32) * width * loudness
    return jnp.minimum(jnp.maximum(result, -bound), bound).astype(held_as)


def setup_inputs(seed: int = 0) -> dict:
    key_list = jax.random.split(jax.random.key(seed), 7)
    query_proj = draw_query_proj(jax.random.fold_in(key_list[6], 71), 0)
    key_proj = draw_key_proj(jax.random.fold_in(key_list[6], 71), 0)
    value_proj = bell_draw(key_list[2], (TOKENS, HEADS * DH), 1.0, 6.0, ((0, 32), (1, 8)))
    query_tangent = bell_draw(key_list[3], (TOKENS, HEADS * DH), 1.0, 6.0, ((0, 32), (1, 8)))
    key_tangent = bell_draw(key_list[4], (TOKENS, HEADS * DH), 1.0, 6.0, ((0, 32), (1, 8)))
    value_tangent = draw_value_tangent(jax.random.fold_in(key_list[6], 71), 0)
    return {"query_proj": query_proj, "key_proj": key_proj, "value_proj": value_proj, "query_tangent": query_tangent, "key_tangent": key_tangent, "value_tangent": value_tangent}


def reference(query_proj, key_proj, value_proj, query_tangent, key_tangent, value_tangent):
    scale_factor = 1.0 / math.sqrt(DH)
    block = math.gcd(TOKENS, 1024)

    def one_head(head_index):

        def columns(arr):
            return lax.dynamic_slice_in_dim(arr, head_index * DH, DH, 1)
        key_h = columns(key_proj)
        value_h = columns(value_proj)
        key_th = columns(key_tangent)
        value_th = columns(value_tangent)
        query_all = columns(query_proj)
        query_tall = columns(query_tangent)

        def one_block(block_index):
            query_h = lax.dynamic_slice_in_dim(query_all, block_index * block, block, 0)
            query_th = lax.dynamic_slice_in_dim(query_tall, block_index * block, block, 0)
            scores = jnp.dot(query_h, key_h.T, preferred_element_type=jnp.float32) * scale_factor
            score_tan = (jnp.dot(query_th, key_h.T, preferred_element_type=jnp.float32) + jnp.dot(query_h, key_th.T, preferred_element_type=jnp.float32)) * scale_factor
            weights = jnp.exp(scores - lax.optimization_barrier(jnp.max(scores, axis=1, keepdims=True)))
            total = lax.optimization_barrier(jnp.sum(weights, axis=1, keepdims=True))
            tilted = weights * score_tan
            cross = lax.optimization_barrier(jnp.sum(tilted, axis=1, keepdims=True))
            weight_bf = weights.astype(jnp.bfloat16)
            tilted_bf = tilted.astype(jnp.bfloat16)
            primal_sum = jnp.dot(weight_bf, value_h, preferred_element_type=jnp.float32)
            shift_sum = jnp.dot(tilted_bf, value_h, preferred_element_type=jnp.float32)
            direct_sum = jnp.dot(weight_bf, value_th, preferred_element_type=jnp.float32)
            primal_out = primal_sum / total
            tangent_out = (shift_sum + direct_sum) / total - cross / total * primal_out
            return (primal_out, tangent_out)
        return lax.map(one_block, jnp.arange(TOKENS // block, dtype=jnp.int32))
    primal_all, tangent_all = lax.map(one_head, jnp.arange(HEADS, dtype=jnp.int32))
    primal_rows = primal_all.transpose(1, 2, 0, 3).reshape(TOKENS, HEADS * DH)
    tangent_rows = tangent_all.transpose(1, 2, 0, 3).reshape(TOKENS, HEADS * DH)
    rms = jnp.sqrt(lax.optimization_barrier(jnp.mean(tangent_rows * tangent_rows, axis=1, keepdims=True)) + 1e-06)
    return (primal_rows.astype(jnp.bfloat16), (tangent_rows / rms).astype(jnp.bfloat16))
```

```python
import functools
import math

import jax
import jax.numpy as jnp
from jax import lax
from jax.experimental import pallas as pl
from jax.experimental.pallas import tpu as pltpu
from jax.sharding import Mesh
from jax.sharding import PartitionSpec as P

HEADS = 16
DH = 128
SCALE = 1.0 / math.sqrt(DH)
LOG2E = math.log2(math.e)
F32 = jnp.float32
BF16 = jnp.bfloat16
MIB = 1 << 20
SWAP = ((0, 1), (1, 0))


def params(limit):
    return pltpu.CompilerParams(vmem_limit_bytes=limit * MIB)


def pack_kernel(q, k, v, qt, kt, vt, own_kv, own_q, other_kv, other_q):
    flip = lax.axis_index("yh") == 1
    spots = ((kt, 0, 0), (k, 0, 1), (v, 0, 2), (vt, 0, 3), (q, 1, 0), (qt, 1, 1))
    for ref, which, at in spots:
        low, high = ref[:, :DH], ref[:, DH:]
        cols = slice(at * DH, (at + 1) * DH)
        (own_kv, own_q)[which][:, cols] = jnp.where(flip, high, low)
        (other_kv, other_q)[which][:, cols] = jnp.where(flip, low, high)


def pack(*arrays):
    rows = arrays[0].shape[0]
    kv = jax.ShapeDtypeStruct((rows, 4 * DH), BF16)
    qq = jax.ShapeDtypeStruct((rows, 2 * DH), BF16)
    return pl.pallas_call(
        pack_kernel,
        out_shape=(kv, qq, kv, qq),
        compiler_params=params(16),
        cost_estimate=pl.CostEstimate(flops=0, bytes_accessed=12 * rows * 2 * DH * 2, transcendentals=0),
        name="pack",
    )(*arrays)


def nt(a, b):
    return lax.dot_general(a, b, (((1,), (1,)), ((), ())), preferred_element_type=F32)


def nn(a, b):
    return lax.dot_general(a, b, (((1,), (0,)), ((), ())), preferred_element_type=F32)


def attend_kernel(blocks, first, last, tiles, *refs):
    q_ref = refs[0]
    kv_refs = refs[1 : 1 + blocks]
    at = 1 + blocks
    if not first:
        acc_ref, stat_ref = refs[at : at + 2]
        at += 2
    outs = refs[at:-1]
    kv = refs[-1]
    rows = kv_refs[0].shape[0]
    step = pl.program_id(0)

    @pl.when(step == 0)
    def _():
        for i, ref in enumerate(kv_refs):
            kv[i * rows : (i + 1) * rows, :] = ref[...]

    query = q_ref[...]
    scores = nt(query[:, :DH], kv[:, DH : 2 * DH]) * (SCALE * LOG2E)
    tangent = nt(query, kv[:, : 2 * DH])
    top = jnp.max(scores, axis=1, keepdims=True)
    if not first:
        old_top = stat_ref[:, 0:1]
        top = jnp.maximum(top, old_top)
    weights = jnp.exp2(scores - top)
    tilted = weights * tangent
    total = jnp.sum(weights, axis=1, keepdims=True)
    cross = jnp.sum(tilted, axis=1, keepdims=True)
    both = nn(weights.astype(BF16), kv[:, 2 * DH :])
    shift = nn(tilted.astype(BF16), kv[:, 2 * DH : 3 * DH]) * SCALE
    primal = both[:, :DH]
    moved = both[:, DH:] + shift
    if not first:
        factor = jnp.exp2(old_top - top)
        total = total + stat_ref[:, 1:2] * factor
        cross = cross + stat_ref[:, 2:3] * factor
        primal = primal + acc_ref[:, :DH] * factor
        moved = moved + acc_ref[:, DH:] * factor
    lane = lax.broadcasted_iota(jnp.int32, (query.shape[0], DH), 1)
    if last:
        near, near_stat, far, far_stat = outs
        inverse = 1.0 / total
        primal = primal * inverse
        moved = moved * inverse
        stat = jnp.where(lane == 0, top + jnp.log2(total), cross * (SCALE * inverse))

        @pl.when(step < tiles // 2)
        def _():
            near[:, :DH] = primal
            near[:, DH:] = moved
            near_stat[...] = stat

        @pl.when(step >= tiles // 2)
        def _():
            far[:, :DH] = primal.astype(BF16)
            far[:, DH:] = moved.astype(BF16)
            far_stat[...] = stat
    else:
        acc, stats = outs
        acc[:, :DH] = primal
        acc[:, DH:] = moved
        stats[...] = jnp.where(lane == 0, top, jnp.where(lane == 1, total, cross))


def attend(query, kvs, state, last=False, tile=256):
    rows = query.shape[0]
    tiles = rows // tile
    keys = sum(kv.shape[0] for kv in kvs)
    row_block = lambda width: pl.BlockSpec((tile, width), lambda i: (i, 0))
    whole = lambda a: pl.BlockSpec(a.shape, lambda i: (0, 0), pipeline_mode=pl.Buffered(1))
    ins = [query, *kvs]
    in_specs = [row_block(2 * DH)] + [whole(kv) for kv in kvs]
    if state is not None:
        ins += state
        in_specs += [row_block(2 * DH), row_block(DH)]
    if last:
        half = tiles // 2
        shapes = [((rows // 2, 2 * DH), F32), ((rows // 2, DH), F32)]
        shapes += [((rows // 2, 2 * DH), BF16), ((rows // 2, DH), F32)]
        near = lambda i: (jnp.minimum(i, half - 1), 0)
        far = lambda i: (jnp.maximum(i - half, 0), 0)
        out_specs = [
            pl.BlockSpec((tile, s[1]), near if n < 2 else far) for n, (s, _) in enumerate(shapes)
        ]
    else:
        shapes = [((rows, 2 * DH), F32), ((rows, DH), F32)]
        out_specs = [row_block(2 * DH), row_block(DH)]
    return pl.pallas_call(
        functools.partial(attend_kernel, len(kvs), state is None, last, tiles),
        grid=(tiles,),
        in_specs=in_specs,
        out_specs=out_specs,
        out_shape=[jax.ShapeDtypeStruct(s, t) for s, t in shapes],
        scratch_shapes=[pltpu.VMEM((keys, 4 * DH), BF16)],
        compiler_params=params(48),
        cost_estimate=pl.CostEstimate(
            flops=2 * 8 * rows * keys * DH,
            bytes_accessed=keys * 4 * DH * 2 + rows * 4 * DH * 8,
            transcendentals=rows * keys,
        ),
        name="attend",
    )(*ins)


def join_kernel(mine, mine_stat, other, other_stat, primal, tangent, squares):
    top_a, top_b = mine_stat[:, 0:1], other_stat[:, 0:1]
    top = jnp.maximum(top_a, top_b)
    part_a, part_b = jnp.exp2(top_a - top), jnp.exp2(top_b - top)
    inverse = 1.0 / (part_a + part_b)
    part_a, part_b = part_a * inverse, part_b * inverse
    both = mine[...] * part_a + other[...].astype(F32) * part_b
    cross = mine_stat[:, 1:2] * part_a + other_stat[:, 1:2] * part_b
    out = both[:, :DH]
    moved = both[:, DH:] - cross * out
    primal[...] = out.astype(BF16)
    tangent[...] = moved
    squares[...] = lax.dot_general(
        jnp.ones((8, DH), F32),
        moved * moved,
        (((1,), (1,)), ((), ())),
        precision=lax.Precision.HIGHEST,
        preferred_element_type=F32,
    )


def join(mine, mine_stat, other, other_stat):
    rows = mine.shape[0]
    half = rows // 2
    row = lambda width: pl.BlockSpec((half, width), lambda i: (i, 0))
    return pl.pallas_call(
        join_kernel,
        grid=(2,),
        in_specs=[row(2 * DH), row(DH), row(2 * DH), row(DH)],
        out_specs=[row(DH), row(DH), pl.BlockSpec((8, half), lambda i: (0, i))],
        out_shape=[
            jax.ShapeDtypeStruct((rows, DH), BF16),
            jax.ShapeDtypeStruct((rows, DH), F32),
            jax.ShapeDtypeStruct((8, rows), F32),
        ],
        compiler_params=params(16),
        name="join",
    )(mine, mine_stat, other, other_stat)


def finish_kernel(primal, primal_in, tangent, tangent_in, square_a, square_b, square_c, square_d, attended, unit):
    flip = lax.axis_index("yh") == 1
    squares = square_a[...] + square_b[...] + square_c[...] + square_d[...]
    mean = lax.dot_general(
        squares,
        jnp.full((8, DH), 1.0 / (8 * HEADS * DH), F32),
        (((0,), (0,)), ((), ())),
        precision=lax.Precision.HIGHEST,
        preferred_element_type=F32,
    )
    inverse = 1.0 / jnp.sqrt(mean + 1e-06)
    mine, other = primal[...], primal_in[...]
    attended[:, :DH] = jnp.where(flip, other, mine)
    attended[:, DH:] = jnp.where(flip, mine, other)
    mine = (tangent[...] * inverse).astype(BF16)
    other = (tangent_in[...] * inverse).astype(BF16)
    unit[:, :DH] = jnp.where(flip, other, mine)
    unit[:, DH:] = jnp.where(flip, mine, other)


def finish(*arrays):
    rows = arrays[0].shape[0]
    out = jax.ShapeDtypeStruct((rows, 2 * DH), BF16)
    return pl.pallas_call(
        finish_kernel, out_shape=(out, out), compiler_params=params(16), name="finish"
    )(*arrays)


def shift(array, axis, count, by):
    return lax.ppermute(array, axis, [(i, (i + by) % count) for i in range(count)])


def on_device(ring, lanes, q, k, v, qt, kt, vt):
    tokens = q.shape[0]
    right = lambda a: shift(a, "z", ring, 1)
    left = lambda a: shift(a, "z", ring, -1)
    over_y = lambda a: lax.ppermute(a, "yh", SWAP)
    over_core = lambda a: lax.ppermute(a, "core", SWAP)

    kv_a, q_a, kv_other, q_other = pack(q, k, v, qt, kt, vt)
    q_b = over_y(q_other)
    kv_b = over_y(kv_other)
    query = jnp.concatenate([q_a, q_b, over_core(q_a), over_core(q_b)], axis=0)

    groups = [[kv_a, kv_b]]
    right_a, left_a, right_b, left_b = kv_a, kv_a, kv_b, kv_b
    for hop in range(1, ring // 2):
        right_a, left_a = right(right_a), left(left_a)
        right_b, left_b = right(right_b), left(left_b)
        groups.append([right_a, left_a, right_b, left_b])
    groups.append([right(right_a), left(left_b)])

    state = None
    for group in groups[:-1]:
        state = attend(query, group, state)
    near, near_stat, far, far_stat = attend(query, groups[-1], state, last=True)
    primal, tangent, squares = join(near, near_stat, over_core(far), over_core(far_stat))

    primal_in = over_y(primal[tokens:])
    tangent_in = over_y(tangent[tokens:])
    squares = squares + shift(squares, "x", lanes, 1) + shift(squares, "x", lanes, 2) + shift(squares, "x", lanes, 3)
    near_sq, far_sq = squares[:, :tokens], squares[:, tokens:]
    same = lax.ppermute(near_sq, "yl", SWAP)
    cross = over_y(far_sq)
    both = lax.ppermute(far_sq, ("yh", "yl"), ((0, 3), (3, 0), (1, 2), (2, 1)))
    return finish(primal[:tokens], primal_in, tangent[:tokens], tangent_in, near_sq, same, cross, both)


def solution(mesh):
    fine = Mesh(mesh.devices.reshape(2, -1, 2, 2, mesh.shape["head"] // 2), ("yh", "z", "core", "yl", "x"))
    spec = P(("yh", "z", "core"), ("yl", "x"))
    return jax.shard_map(
        functools.partial(on_device, fine.shape["z"], fine.shape["x"]),
        mesh=fine,
        in_specs=(spec,) * 6,
        out_specs=(spec, spec),
        check_vma=False,
    )
```

```python
import functools
import math

import jax
import jax.numpy as jnp
from jax import lax
from jax.experimental import pallas as pl
from jax.experimental.pallas import tpu as pltpu
from jax.sharding import Mesh
from jax.sharding import PartitionSpec as P

HEADS = 16
DH = 128
SCALE = 1.0 / math.sqrt(DH)
LOG2E = math.log2(math.e)
LIMIT = 2.0**40
F32 = jnp.float32
BF16 = jnp.bfloat16
SWAP = ((0, 1), (1, 0))
PARAMS = pltpu.CompilerParams(vmem_limit_bytes=60 << 20)


def nt(a, b):
    return lax.dot_general(a, b, (((1,), (1,)), ((), ())), preferred_element_type=F32)


def nn(a, b):
    return lax.dot_general(a, b, (((1,), (0,)), ((), ())), preferred_element_type=F32)


def pack_kernel(q, k, v, qt, kt, vt, own, other, sems):
    rows = q.shape[0]
    half = rows // 2
    yh = lax.axis_index("yh")
    copies = []
    for which, out in enumerate((own, other)):
        head = yh if which == 0 else 1 - yh
        cols = pl.ds(pl.multiple_of(head * DH, DH), DH)
        for at, ref in enumerate((kt, k, v, vt)):
            copies.append((ref.at[:, cols], out.at[0:rows, at * DH : (at + 1) * DH]))
        for at, ref in enumerate((q, qt, q, qt)):
            part = slice(0, half) if at < 2 else slice(half, rows)
            copies.append((ref.at[part, cols], out.at[rows : rows + half, at * DH : (at + 1) * DH]))
    copies = [pltpu.make_async_copy(a, b, sems.at[i]) for i, (a, b) in enumerate(copies)]
    for copy in copies:
        copy.start()
    for copy in copies:
        copy.wait()


def pack(*arrays):
    rows = arrays[0].shape[0]
    out = jax.ShapeDtypeStruct((rows + rows // 2, 4 * DH), BF16)
    return pl.pallas_call(
        pack_kernel,
        out_shape=(out, out),
        in_specs=[pl.BlockSpec(memory_space=pl.ANY)] * 6,
        out_specs=[pl.BlockSpec(memory_space=pl.ANY)] * 2,
        scratch_shapes=[pltpu.SemaphoreType.DMA((16,))],
        compiler_params=PARAMS,
        cost_estimate=pl.CostEstimate(flops=0, bytes_accessed=12 * rows * 2 * DH * 2, transcendentals=0),
        name="pack",
    )(*arrays)


def lanes(x):
    out = x[:, :DH]
    for i in range(1, x.shape[1] // DH):
        out = out + x[:, i * DH : (i + 1) * DH]
    return out


def wide(x, times):
    return jnp.concatenate([x] * times, axis=1)


def part(query, kv, state, exact):
    keys = kv.shape[0]
    scores = nt(query[:, :DH], kv[:, DH : 2 * DH]) * (SCALE * LOG2E)
    tangent = nt(query, kv[:, : 2 * DH])
    old = state
    if exact:
        top = jnp.broadcast_to(jnp.max(scores, axis=1, keepdims=True), (query.shape[0], DH))
        if old is not None:
            top = jnp.maximum(top, old[4])
    else:
        top = old[4]
    weights = jnp.exp2(scores - wide(top, keys // DH))
    tilted = weights * tangent
    total, cross = lanes(weights), lanes(tilted)
    both = nn(weights.astype(BF16), kv[:, 2 * DH :])
    moved = both[:, DH:] + nn(tilted.astype(BF16), kv[:, 2 * DH : 3 * DH]) * SCALE
    new = (both[:, :DH], moved, total, cross)
    if old is None:
        return (*new, top)
    if exact:
        factor = jnp.exp2(old[4] - top)
        return (*(n + o * factor for n, o in zip(new, old[:4])), top)
    return (*(n + o for n, o in zip(new, old[:4])), top)


def read(ref, rows=slice(None)):
    return tuple(ref[rows, i * DH : (i + 1) * DH] for i in range(5))


def write(ref, state, rows=slice(None)):
    for i, piece in enumerate(state):
        ref[rows, i * DH : (i + 1) * DH] = piece


def attend_kernel(blocks, first, last, *refs):
    q_ref = refs[0]
    kv_refs = refs[1 : 1 + blocks]
    at = 1 + blocks
    if not first:
        old_ref = refs[at]
        at += 1
    outs = refs[at : at + (2 if last else 1)]
    kv = refs[at + len(outs)]
    new_ref = refs[-1] if last else outs[0]

    @pl.when(pl.program_id(0) == 0)
    def _():
        at = 0
        for ref in kv_refs:
            kv[at : at + ref.shape[0], :] = ref[...]
            at += ref.shape[0]

    if first:
        write(new_ref, part(q_ref[...], kv, None, True))
    else:
        state = part(q_ref[...], kv, read(old_ref), False)
        write(new_ref, state)
        fine = jnp.max(state[2]) < LIMIT

        @pl.when(jnp.logical_not(fine))
        def _():
            def body(i, carry):
                rows = pl.ds(pl.multiple_of(i * 64, 64), 64)
                write(new_ref, part(q_ref[rows, :], kv, read(old_ref, rows), True), rows)
                return carry

            lax.fori_loop(0, q_ref.shape[0] // 64, body, 0)

    if last:
        out, stats = outs
        primal, moved, total, cross, top = read(new_ref)
        total = jnp.sum(total, axis=1, keepdims=True)
        cross = jnp.sum(cross, axis=1, keepdims=True)
        inverse = 1.0 / total
        out[:, :DH] = (primal * inverse).astype(out.dtype)
        out[:, DH:] = (moved * inverse).astype(out.dtype)
        lane = lax.broadcasted_iota(jnp.int32, top.shape, 1)
        stats[...] = jnp.where(lane == 0, top + jnp.log2(total), cross * (SCALE * inverse))


def attend(query, kvs, state, span=None, kind=None, tile=256):
    begin, end = span or (0, query.shape[0])
    rows = end - begin
    tiles, off = rows // tile, begin // tile
    height = lambda kv: 384 if kv.shape[0] == 576 else kv.shape[0]
    keys = sum(height(kv) for kv in kvs)
    block = lambda width, base: pl.BlockSpec((tile, width), lambda i: (i + base, 0))
    whole = lambda a: pl.BlockSpec((height(a), 4 * DH), lambda i: (0, 0), pipeline_mode=pl.Buffered(1))
    ins = [query, *kvs]
    in_specs = [block(2 * DH, off)] + [whole(kv) for kv in kvs]
    if state is not None:
        ins.append(state)
        in_specs.append(block(5 * DH, off))
    scratch = [pltpu.VMEM((keys, 4 * DH), BF16)]
    if kind is None:
        out_specs = [block(5 * DH, 0)]
        shapes = [jax.ShapeDtypeStruct((rows, 5 * DH), F32)]
    else:
        out_specs = [block(2 * DH, 0), block(DH, 0)]
        shapes = [jax.ShapeDtypeStruct((rows, 2 * DH), kind), jax.ShapeDtypeStruct((rows, DH), F32)]
        scratch.append(pltpu.VMEM((tile, 5 * DH), F32))
    out = pl.pallas_call(
        functools.partial(attend_kernel, len(kvs), state is None, kind is not None),
        grid=(tiles,),
        in_specs=in_specs,
        out_specs=out_specs,
        out_shape=shapes,
        scratch_shapes=scratch,
        compiler_params=PARAMS,
        cost_estimate=pl.CostEstimate(
            flops=2 * 8 * rows * keys * DH,
            bytes_accessed=keys * 4 * DH * 2 + rows * 5 * DH * 8,
            transcendentals=rows * keys,
        ),
        name="attend",
    )(*ins)
    return out if kind is not None else out[0]


def join_kernel(mine, mine_stat, other, other_stat, keep, send, squares):
    step = pl.program_id(0)
    yh = lax.axis_index("yh")
    top_a, top_b = mine_stat[:, 0:1], other_stat[:, 0:1]
    top = jnp.maximum(top_a, top_b)
    part_a, part_b = jnp.exp2(top_a - top), jnp.exp2(top_b - top)
    inverse = 1.0 / (part_a + part_b)
    part_a, part_b = part_a * inverse, part_b * inverse
    both = mine[...] * part_a + other[...].astype(F32) * part_b
    cross = mine_stat[:, 1:2] * part_a + other_stat[:, 1:2] * part_b
    out = both[:, :DH]
    moved = both[:, DH:] - cross * out

    @pl.when(step == 0)
    def _():
        keep[:, :DH] = out
        keep[:, DH:] = moved

    @pl.when(step == 1)
    def _():
        send[:, :DH] = out.astype(BF16)
        send[:, DH:] = moved.astype(BF16)

    owner = jnp.where(step == 0, yh, 1 - yh)
    squares[pl.ds(pl.multiple_of(owner * 8, 8), 8), :] = lax.dot_general(
        jnp.ones((8, DH), F32),
        moved * moved,
        (((1,), (1,)), ((), ())),
        precision=lax.Precision.HIGHEST,
        preferred_element_type=F32,
    )


def join(mine, mine_stat, other, other_stat):
    half = mine.shape[0] // 2
    row = lambda width: pl.BlockSpec((half, width), lambda i: (i, 0))
    fixed = lambda *shape: pl.BlockSpec(shape, lambda i: (0, 0))
    return pl.pallas_call(
        join_kernel,
        grid=(2,),
        in_specs=[row(2 * DH), row(DH), row(2 * DH), row(DH)],
        out_specs=[fixed(half, 2 * DH), fixed(half, 2 * DH), fixed(16, half)],
        out_shape=[
            jax.ShapeDtypeStruct((half, 2 * DH), F32),
            jax.ShapeDtypeStruct((half, 2 * DH), BF16),
            jax.ShapeDtypeStruct((16, half), F32),
        ],
        compiler_params=PARAMS,
        name="join",
    )(mine, mine_stat, other, other_stat)


def finish_kernel(keep, come, squares, attended, unit):
    flip = lax.axis_index("yh") == 1
    mean = lax.dot_general(
        squares[...],
        jnp.full((16, DH), 1.0 / (HEADS * DH), F32),
        (((0,), (0,)), ((), ())),
        precision=lax.Precision.HIGHEST,
        preferred_element_type=F32,
    )
    inverse = 1.0 / jnp.sqrt(mean + 1e-06)
    mine, other = keep[:, :DH].astype(BF16), come[:, :DH]
    attended[:, :DH] = jnp.where(flip, other, mine)
    attended[:, DH:] = jnp.where(flip, mine, other)
    mine = (keep[:, DH:] * inverse).astype(BF16)
    other = (come[:, DH:].astype(F32) * inverse).astype(BF16)
    unit[:, :DH] = jnp.where(flip, other, mine)
    unit[:, DH:] = jnp.where(flip, mine, other)


def finish(*arrays):
    out = jax.ShapeDtypeStruct(arrays[1].shape, BF16)
    return pl.pallas_call(finish_kernel, out_shape=(out, out), compiler_params=PARAMS, name="finish")(*arrays)


def on_device(ring, q, k, v, qt, kt, vt):
    tokens = q.shape[0]
    hop_pairs = [(z * 2 + c, (z + 1 - 2 * c) % ring * 2 + c) for z in range(ring) for c in range(2)]
    hop = lambda a: lax.ppermute(a, ("z", "core"), hop_pairs)
    over_y = lambda a: lax.ppermute(a, "yh", SWAP)
    over_core = lambda a: lax.ppermute(a, "core", SWAP)
    queries = lambda a: (a[tokens:, : 2 * DH], a[tokens:, 2 * DH :])

    own, other = pack(q, k, v, qt, kt, vt)
    peer = over_y(other)
    own_core, peer_core = over_core(own), over_core(peer)
    near_x = jnp.concatenate([own[:tokens], own_core[:tokens]], axis=0)
    far_x = jnp.concatenate([peer[:tokens], peer_core[:tokens]], axis=0)
    query = jnp.concatenate([piece for a in (own, peer, own_core, peer_core) for piece in queries(a)], axis=0)

    near_hops, far_hops = [], []
    for _ in range(ring // 2 - 1):
        near_x, far_x = hop(near_x), hop(far_x)
        near_hops.append(near_x)
        far_hops.append(far_x)
    near_hops.append(hop(near_x[:tokens]))
    far_hops.append(hop(far_x[:tokens]))

    state = attend(query, [own, peer, near_hops[0]], None)
    state = attend(query, [near_hops[1], far_hops[0]], state)
    state = attend(query, [near_hops[2], far_hops[1]], state)
    state = attend(query, [far_hops[2]], state)
    ends = [near_hops[3], far_hops[3]]
    rows = query.shape[0]
    far, far_stat = attend(query, ends, state, (rows // 2, rows), BF16)
    other, other_stat = over_core(far), over_core(far_stat)
    near, near_stat = attend(query, ends, state, (0, rows // 2), F32)
    keep, send, squares = join(near, near_stat, other, other_stat)
    come = over_y(send)
    squares = lax.all_to_all(squares, ("yh", "yl", "x"), 0, 0, tiled=True)
    return finish(keep, come, squares)


def solution(mesh):
    fine = Mesh(mesh.devices.reshape(2, -1, 2, 2, mesh.shape["head"] // 2), ("yh", "z", "core", "yl", "x"))
    spec = P(("yh", "z", "core"), ("yl", "x"))
    return jax.shard_map(
        functools.partial(on_device, fine.shape["z"]),
        mesh=fine,
        in_specs=(spec,) * 6,
        out_specs=(spec, spec),
        check_vma=False,
    )
```

```python
import functools
import math

import jax
import jax.numpy as jnp
from jax import lax
from jax.experimental import pallas as pl
from jax.experimental.pallas import tpu as pltpu
from jax.sharding import Mesh
from jax.sharding import PartitionSpec as P

HEADS = 16
DH = 128
SCALE = 1.0 / math.sqrt(DH)
LOG2E = math.log2(math.e)
LIMIT = 2.0**40
TILE = 256
F32 = jnp.float32
BF16 = jnp.bfloat16
SWAP = ((0, 1), (1, 0))
PARAMS = pltpu.CompilerParams(vmem_limit_bytes=28 << 20)


def nt(a, b):
    return lax.dot_general(a, b, (((1,), (1,)), ((), ())), preferred_element_type=F32)


def nn(a, b):
    return lax.dot_general(a, b, (((1,), (0,)), ((), ())), preferred_element_type=F32)


def pack_kernel(q, k, v, qt, kt, vt, own_kv, own_q, other):
    step = pl.program_id(0)
    flip = lax.axis_index("yh") == 1
    rows = q.shape[0]
    for at, ref in enumerate((kt, k, v, vt, q, qt)):
        low, high = ref[:, :DH], ref[:, DH:]
        mine, theirs = jnp.where(flip, high, low), jnp.where(flip, low, high)
        if at < 4:
            cols = slice(at * DH, (at + 1) * DH)
            own_kv[:, cols] = mine
            other[pl.ds(pl.multiple_of(step * rows, rows), rows), cols] = theirs
        else:
            own_q[:, (at - 4) * DH : (at - 3) * DH] = mine
            for half in range(2):

                @pl.when(step == half)
                def _():
                    first = (2 * half + at - 4) * DH
                    other[2 * rows :, first : first + DH] = theirs


def pack(*arrays):
    rows = arrays[0].shape[0]
    half = rows // 2
    row = lambda width: pl.BlockSpec((half, width), lambda i: (i, 0))
    return pl.pallas_call(
        pack_kernel,
        grid=(2,),
        in_specs=[row(2 * DH)] * 6,
        out_specs=[row(4 * DH), row(2 * DH), pl.BlockSpec((rows + half, 4 * DH), lambda i: (0, 0))],
        out_shape=[
            jax.ShapeDtypeStruct((rows, 4 * DH), BF16),
            jax.ShapeDtypeStruct((rows, 2 * DH), BF16),
            jax.ShapeDtypeStruct((rows + half, 4 * DH), BF16),
        ],
        compiler_params=pltpu.CompilerParams(vmem_limit_bytes=60 << 20),
        cost_estimate=pl.CostEstimate(flops=0, bytes_accessed=12 * rows * 2 * DH * 2, transcendentals=0),
        name="pack",
    )(*arrays)


def lanes(x):
    out = x[:, :DH]
    for i in range(1, x.shape[1] // DH):
        out = out + x[:, i * DH : (i + 1) * DH]
    return out


def wide(x, times):
    return jnp.concatenate([x] * times, axis=1)


def dots(query, kv):
    return nt(query[:, :DH], kv[:, DH : 2 * DH]), nt(query, kv[:, : 2 * DH])


def part(products, kv, old, exact):
    scores, tangent = products
    rows, keys = scores.shape
    scores = scores * (SCALE * LOG2E)
    if exact:
        top = jnp.broadcast_to(jnp.max(scores, axis=1, keepdims=True), (rows, DH))
        if old is not None:
            top = jnp.maximum(top, old[4])
    else:
        top = old[4]
    weights = jnp.exp2(scores - wide(top, keys // DH))
    tilted = weights * tangent
    total, cross = lanes(weights), lanes(tilted)
    both = nn(weights.astype(BF16), kv[:, 2 * DH :])
    moved = both[:, DH:] + nn(tilted.astype(BF16), kv[:, 2 * DH : 3 * DH]) * SCALE
    new = (both[:, :DH], moved, total, cross)
    if old is None:
        return (*new, top)
    if exact:
        factor = jnp.exp2(old[4] - top)
        return (*(n + o * factor for n, o in zip(new, old[:4])), top)
    return (*(n + o for n, o in zip(new, old[:4])), top)


def read(ref, rows):
    return tuple(ref[rows, i * DH : (i + 1) * DH] for i in range(5))


def write(ref, state, rows):
    for i, piece in enumerate(state):
        ref[rows, i * DH : (i + 1) * DH] = piece


def begin_kernel(own_kv, own_q, own_core_q, peer, peer_core, state, query, kv):
    rows = own_kv.shape[0]
    half = rows // 2
    kv[:rows, :] = own_kv[...]
    kv[rows:, :] = peer[:rows, :]
    query[:rows, :] = own_q[...]
    query[2 * rows : 3 * rows, :] = own_core_q[...]
    for at, ref in ((rows, peer), (3 * rows, peer_core)):
        query[at : at + half, :] = ref[rows:, : 2 * DH]
        query[at + half : at + rows, :] = ref[rows:, 2 * DH :]
    spans = [slice(i, i + TILE) for i in range(0, query.shape[0], TILE)]
    ahead = dots(query[spans[0], :], kv)
    for i, span in enumerate(spans):
        now = ahead
        if i + 1 < len(spans):
            ahead = dots(query[spans[i + 1], :], kv)
        write(state, part(now, kv, None, True), span)


def attend_kernel(blocks, base, last, q_ref, *refs):
    kv_refs = refs[:blocks]
    old_ref = refs[blocks]
    outs = refs[blocks + 1 : blocks + (3 if last else 2)]
    rest = list(refs[blocks + 1 + len(outs) :])
    kv = kv_refs[0]
    if blocks > 1:
        kv = rest.pop(0)
        at = 0
        for ref in kv_refs:
            kv[at : at + ref.shape[0], :] = ref[...]
            at += ref.shape[0]
    new_ref = rest.pop(0) if last else outs[0]
    rows = new_ref.shape[0]
    starts = list(range(0, rows, TILE))
    query = lambda at, size: q_ref[pl.ds(base + at, size), :]
    ahead = dots(query(0, TILE), kv)
    worst = None
    for i, at in enumerate(starts):
        now = ahead
        if i + 1 < len(starts):
            ahead = dots(query(starts[i + 1], TILE), kv)
        state = part(now, kv, read(old_ref, slice(base + at, base + at + TILE)), False)
        write(new_ref, state, slice(at, at + TILE))
        peak = jnp.max(state[2].reshape(TILE // 8, 8, DH), axis=0)
        worst = peak if worst is None else jnp.maximum(worst, peak)

    @pl.when(jnp.logical_not(jnp.max(worst) < LIMIT))
    def _():
        def body(i, carry):
            at = pl.multiple_of(i * 64, 64)
            here, there = pl.ds(at, 64), pl.ds(base + at, 64)
            write(new_ref, part(dots(q_ref[there, :], kv), kv, read(old_ref, there), True), here)
            return carry

        lax.fori_loop(0, rows // 64, body, 0)

    if last:
        out, stats = outs
        primal, moved, total, cross, top = read(new_ref, slice(0, rows))
        total = jnp.sum(total, axis=1, keepdims=True)
        cross = jnp.sum(cross, axis=1, keepdims=True)
        inverse = 1.0 / total
        out[:, :DH] = (primal * inverse).astype(out.dtype)
        out[:, DH:] = (moved * inverse).astype(out.dtype)
        lane = lax.broadcasted_iota(jnp.int32, top.shape, 1)
        stats[...] = jnp.where(lane == 0, top + jnp.log2(total), cross * (SCALE * inverse))


def cost(rows, keys):
    return pl.CostEstimate(
        flops=2 * 8 * rows * keys * DH, bytes_accessed=keys * 4 * DH * 2, transcendentals=rows * keys
    )


def begin(*arrays):
    rows, keys = 4 * arrays[0].shape[0], 2 * arrays[0].shape[0]
    return pl.pallas_call(
        begin_kernel,
        out_shape=[jax.ShapeDtypeStruct((rows, 5 * DH), F32), jax.ShapeDtypeStruct((rows, 2 * DH), BF16)],
        scratch_shapes=[pltpu.VMEM((keys, 4 * DH), BF16)],
        compiler_params=PARAMS,
        cost_estimate=cost(rows, keys),
        name="begin",
    )(*arrays)


def attend(query, kvs, state, span=None, kind=None):
    base, end = span or (0, query.shape[0])
    rows = end - base
    keys = sum(kv.shape[0] for kv in kvs)
    scratch = [pltpu.VMEM((keys, 4 * DH), BF16)] if len(kvs) > 1 else []
    if kind is None:
        shapes = jax.ShapeDtypeStruct((rows, 5 * DH), F32)
    else:
        shapes = [jax.ShapeDtypeStruct((rows, 2 * DH), kind), jax.ShapeDtypeStruct((rows, DH), F32)]
        scratch.append(pltpu.VMEM((rows, 5 * DH), F32))
    return pl.pallas_call(
        functools.partial(attend_kernel, len(kvs), base, kind is not None),
        out_shape=shapes,
        scratch_shapes=scratch,
        compiler_params=PARAMS,
        cost_estimate=cost(rows, keys),
        name="attend",
    )(query, *kvs, state)


def join_kernel(mine, mine_stat, other, other_stat, keep, send, squares):
    yh = lax.axis_index("yh")
    half = keep.shape[0]
    for step, rows in enumerate((slice(0, half), slice(half, 2 * half))):
        top_a, top_b = mine_stat[rows, 0:1], other_stat[rows, 0:1]
        top = jnp.maximum(top_a, top_b)
        part_a, part_b = jnp.exp2(top_a - top), jnp.exp2(top_b - top)
        inverse = 1.0 / (part_a + part_b)
        part_a, part_b = part_a * inverse, part_b * inverse
        both = mine[rows, :] * part_a + other[rows, :].astype(F32) * part_b
        cross = mine_stat[rows, 1:2] * part_a + other_stat[rows, 1:2] * part_b
        out = both[:, :DH]
        moved = both[:, DH:] - cross * out
        kept = (keep, send)[step]
        kept[:, :DH] = out.astype(kept.dtype)
        kept[:, DH:] = moved.astype(kept.dtype)
        sums = lax.dot_general(
            jnp.ones((8, DH), F32),
            moved * moved,
            (((1,), (1,)), ((), ())),
            precision=lax.Precision.HIGHEST,
            preferred_element_type=F32,
        )
        row = lax.broadcasted_iota(jnp.int32, (8, DH), 0)
        slab = jnp.zeros((8, DH), F32)
        for i in range(half // DH):
            slab = jnp.where(row == i, sums[:, i * DH : (i + 1) * DH], slab)
        owner = yh if step == 0 else 1 - yh
        for i in range(8):
            squares[owner * 8 + i] = slab


def join(*arrays):
    half = arrays[0].shape[0] // 2
    return pl.pallas_call(
        join_kernel,
        out_shape=[
            jax.ShapeDtypeStruct((half, 2 * DH), F32),
            jax.ShapeDtypeStruct((half, 2 * DH), BF16),
            jax.ShapeDtypeStruct((16, 8, DH), F32),
        ],
        compiler_params=PARAMS,
        name="join",
    )(*arrays)


def finish_kernel(keep, come, squares, attended, unit):
    flip = lax.axis_index("yh") == 1
    sums = squares[0]
    for i in range(1, 16):
        sums = sums + squares[i]
    row = lax.broadcasted_iota(jnp.int32, (8, DH), 0)
    for i in range(keep.shape[0] // DH):
        rows = slice(i * DH, (i + 1) * DH)
        mean = lax.dot_general(
            jnp.where(row == i, sums, 0.0),
            jnp.full((8, DH), 1.0 / (HEADS * DH), F32),
            (((0,), (0,)), ((), ())),
            precision=lax.Precision.HIGHEST,
            preferred_element_type=F32,
        )
        inverse = 1.0 / jnp.sqrt(mean + 1e-06)
        mine, other = keep[rows, :DH].astype(BF16), come[rows, :DH]
        attended[rows, :DH] = jnp.where(flip, other, mine)
        attended[rows, DH:] = jnp.where(flip, mine, other)
        mine = (keep[rows, DH:] * inverse).astype(BF16)
        other = (come[rows, DH:].astype(F32) * inverse).astype(BF16)
        unit[rows, :DH] = jnp.where(flip, other, mine)
        unit[rows, DH:] = jnp.where(flip, mine, other)


def finish(*arrays):
    out = jax.ShapeDtypeStruct(arrays[1].shape, BF16)
    return pl.pallas_call(finish_kernel, out_shape=(out, out), compiler_params=PARAMS, name="finish")(*arrays)


def on_device(ring, q, k, v, qt, kt, vt):
    tokens = q.shape[0]
    hop_pairs = [(z * 2 + c, (z + 1 - 2 * c) % ring * 2 + c) for z in range(ring) for c in range(2)]
    hop = lambda a: lax.ppermute(a, ("z", "core"), hop_pairs)
    over_y = lambda a: lax.ppermute(a, "yh", SWAP)
    over_core = lambda a: lax.ppermute(a, "core", SWAP)
    def after(block, state):
        return lax.optimization_barrier((block, state))

    own_kv, own_q, other = pack(q, k, v, qt, kt, vt)
    peer = over_y(other)
    near = hop(jnp.concatenate([own_kv, over_core(own_kv)], axis=0))
    own_core_q = over_core(own_q)
    peer_core = over_core(peer)
    far = hop(jnp.concatenate([peer[:tokens], peer_core[:tokens]], axis=0))
    state, query = begin(own_kv, own_q, own_core_q, peer, peer_core)
    near_next = hop(near)
    state = attend(query, [near], state)
    near, state = after(near_next, state)
    near_next = hop(near)
    state = attend(query, [near], state)
    far, state = after(far, state)
    far_next = hop(far)
    state = attend(query, [far], state)
    near, state = after(near_next, state)
    near_next = hop(near[:tokens])
    state = attend(query, [near], state)
    far, state = after(far_next, state)
    far_next = hop(far)
    state = attend(query, [far], state)
    far, state = after(far_next, state)
    far_next = hop(far[:tokens])
    state = attend(query, [far, near_next], state)
    rows = query.shape[0]
    there, there_stat = attend(query, [far_next], state, (rows // 2, rows), BF16)
    come, come_stat = over_core(there), over_core(there_stat)
    here, here_stat = attend(query, [far_next], state, (0, rows // 2), F32)
    keep, send, squares = join(here, here_stat, come, come_stat)
    come = over_y(send)
    squares = lax.all_to_all(squares, ("yh", "yl", "x"), 0, 0, tiled=True)
    return finish(keep, come, squares)


def solution(mesh):
    fine = Mesh(mesh.devices.reshape(2, -1, 2, 2, mesh.shape["head"] // 2), ("yh", "z", "core", "yl", "x"))
    spec = P(("yh", "z", "core"), ("yl", "x"))
    return jax.shard_map(
        functools.partial(on_device, fine.shape["z"]),
        mesh=fine,
        in_specs=(spec,) * 6,
        out_specs=(spec, spec),
        check_vma=False,
    )
```

```python
import functools
import math

import jax
import jax.numpy as jnp
from jax import lax
from jax.experimental import pallas as pl
from jax.experimental.pallas import tpu as pltpu
from jax.sharding import Mesh
from jax.sharding import PartitionSpec as P

HEADS = 16
DH = 128
SCALE = 1.0 / math.sqrt(DH)
LOG2E = math.log2(math.e)
LIMIT = 2.0**40
TILE = 256
SMALL = 128
F32 = jnp.float32
BF16 = jnp.bfloat16
SWAP = ((0, 1), (1, 0))
PARAMS = pltpu.CompilerParams(vmem_limit_bytes=28 << 20)


def nt(a, b):
    return lax.dot_general(a, b, (((1,), (1,)), ((), ())), preferred_element_type=F32)


def nn(a, b):
    return lax.dot_general(a, b, (((1,), (0,)), ((), ())), preferred_element_type=F32)


def pack_kernel(q, k, v, qt, kt, vt, own_kv, own_q, other_kv, other_q):
    flip = lax.axis_index("yh") == 1
    spots = ((kt, 0, 0), (k, 0, 1), (v, 0, 2), (vt, 0, 3), (q, 1, 0), (qt, 1, 1))
    for ref, which, at in spots:
        low, high = ref[:, :DH], ref[:, DH:]
        cols = slice(at * DH, (at + 1) * DH)
        (own_kv, own_q)[which][:, cols] = jnp.where(flip, high, low)
        (other_kv, other_q)[which][:, cols] = jnp.where(flip, low, high)


def pack(*arrays):
    rows = arrays[0].shape[0]
    row = lambda width: pl.BlockSpec((rows // 2, width), lambda i: (i, 0))
    shapes = [jax.ShapeDtypeStruct((rows, n * DH), BF16) for n in (4, 2, 4, 2)]
    return pl.pallas_call(
        pack_kernel,
        grid=(2,),
        in_specs=[row(2 * DH)] * 6,
        out_specs=[row(n * DH) for n in (4, 2, 4, 2)],
        out_shape=shapes,
        compiler_params=pltpu.CompilerParams(vmem_limit_bytes=60 << 20),
        cost_estimate=pl.CostEstimate(flops=0, bytes_accessed=12 * rows * 2 * DH * 2, transcendentals=0),
        name="pack",
    )(*arrays)


def lanes(x):
    out = x[:, :DH]
    for i in range(1, x.shape[1] // DH):
        out = out + x[:, i * DH : (i + 1) * DH]
    return out


def wide(x, times):
    return jnp.concatenate([x] * times, axis=1)


def dots(query, kv):
    return nt(query[:, :DH], kv[:, DH : 2 * DH]), nt(query, kv[:, : 2 * DH])


def part(products, kv, old, exact):
    scores, tangent = products
    rows, keys = scores.shape
    scores = scores * (SCALE * LOG2E)
    if exact:
        top = jnp.broadcast_to(jnp.max(scores, axis=1, keepdims=True), (rows, DH))
        if old is not None:
            top = jnp.maximum(top, old[4])
    else:
        top = old[4]
    weights = jnp.exp2(scores - wide(top, keys // DH))
    tilted = weights * tangent
    total, cross = lanes(weights), lanes(tilted)
    both = nn(weights.astype(BF16), kv[:, 2 * DH :])
    moved = both[:, DH:] + nn(tilted.astype(BF16), kv[:, 2 * DH : 3 * DH]) * SCALE
    new = (both[:, :DH], moved, total, cross)
    if old is None:
        return (*new, top)
    if exact:
        factor = jnp.exp2(old[4] - top)
        return (*(n + o * factor for n, o in zip(new, old[:4])), top)
    return (*(n + o for n, o in zip(new, old[:4])), top)


def read(ref, rows):
    return tuple(ref[rows, i * DH : (i + 1) * DH] for i in range(5))


def write(ref, state, rows):
    for i, piece in enumerate(state):
        ref[rows, i * DH : (i + 1) * DH] = piece


def begin_kernel(own_kv, peer_kv, own_q, core_q, state, query, kv):
    rows = own_kv.shape[0]
    kv[:rows, :] = own_kv[...]
    kv[rows:, :] = peer_kv[...]
    query[: 2 * rows, :] = own_q[...]
    query[2 * rows :, :] = core_q[...]

    def body(i, carry):
        at = pl.multiple_of(i * 2 * TILE, 2 * TILE)
        spans = [pl.ds(at, TILE), pl.ds(at + TILE, TILE)]
        products = [dots(query[span, :], kv) for span in spans]
        for span, product in zip(spans, products):
            write(state, part(product, kv, None, True), span)
        return carry

    lax.fori_loop(0, query.shape[0] // (2 * TILE), body, 0)


def attend_kernel(blocks, base, last, q_ref, *refs):
    kv_refs = refs[:blocks]
    old_ref = refs[blocks]
    outs = refs[blocks + 1 : blocks + (3 if last else 2)]
    rest = list(refs[blocks + 1 + len(outs) :])
    kv = kv_refs[0]
    if blocks > 1:
        kv = rest.pop(0)
        at = 0
        for ref in kv_refs:
            kv[at : at + ref.shape[0], :] = ref[...]
            at += ref.shape[0]
    new_ref = rest.pop(0) if last else outs[0]
    rows, keys = new_ref.shape[0], kv.shape[0]
    each = 2 if rows % (2 * TILE) == 0 else rows // TILE

    def body(i, worst):
        starts = [pl.multiple_of(i * each * TILE, TILE) + n * TILE for n in range(each)]
        ahead = dots(q_ref[pl.ds(base + starts[0], TILE), :], kv)
        for n, at in enumerate(starts):
            now = ahead
            if n + 1 < each:
                ahead = dots(q_ref[pl.ds(base + starts[n + 1], TILE), :], kv)
            state = part(now, kv, read(old_ref, pl.ds(base + at, TILE)), False)
            write(new_ref, state, pl.ds(at, TILE))
            worst = jnp.maximum(worst, jnp.max(state[2].reshape(TILE // 8, 8, DH), axis=0))
        return worst

    worst = lax.fori_loop(0, rows // (each * TILE), body, jnp.zeros((8, DH), F32))

    @pl.when(jnp.logical_not(jnp.max(worst) < LIMIT))
    def _():
        def again(i, carry):
            at = pl.multiple_of(i * SMALL, SMALL)
            here, there = pl.ds(at, SMALL), pl.ds(base + at, SMALL)
            new_ref[here, :] = old_ref[there, :]

            def some(j, inner):
                block = kv[pl.ds(pl.multiple_of(j * 3 * DH, 3 * DH), 3 * DH), :]
                write(new_ref, part(dots(q_ref[there, :], block), block, read(new_ref, here), True), here)
                return inner

            return lax.fori_loop(0, keys // (3 * DH), some, carry)

        lax.fori_loop(0, rows // SMALL, again, 0)

    if last:
        out, stats = outs
        primal, moved, total, cross, top = read(new_ref, slice(0, rows))
        total = jnp.sum(total, axis=1, keepdims=True)
        cross = jnp.sum(cross, axis=1, keepdims=True)
        inverse = 1.0 / total
        out[:, :DH] = (primal * inverse).astype(out.dtype)
        out[:, DH:] = (moved * inverse).astype(out.dtype)
        lane = lax.broadcasted_iota(jnp.int32, top.shape, 1)
        stats[...] = jnp.where(lane == 0, top + jnp.log2(total), cross * (SCALE * inverse))


def cost(rows, keys):
    return pl.CostEstimate(
        flops=2 * 8 * rows * keys * DH, bytes_accessed=keys * 4 * DH * 2, transcendentals=rows * keys
    )


def begin(*arrays):
    rows, keys = 4 * arrays[0].shape[0], 2 * arrays[0].shape[0]
    return pl.pallas_call(
        begin_kernel,
        out_shape=[jax.ShapeDtypeStruct((rows, 5 * DH), F32), jax.ShapeDtypeStruct((rows, 2 * DH), BF16)],
        scratch_shapes=[pltpu.VMEM((keys, 4 * DH), BF16)],
        compiler_params=PARAMS,
        cost_estimate=cost(rows, keys),
        name="begin",
    )(*arrays)


def attend(query, kvs, state, span=None, kind=None):
    base, end = span or (0, query.shape[0])
    rows = end - base
    keys = sum(kv.shape[0] for kv in kvs)
    scratch = [pltpu.VMEM((keys, 4 * DH), BF16)] if len(kvs) > 1 else []
    if kind is None:
        shapes = jax.ShapeDtypeStruct((rows, 5 * DH), F32)
    else:
        shapes = [jax.ShapeDtypeStruct((rows, 2 * DH), kind), jax.ShapeDtypeStruct((rows, DH), F32)]
        scratch.append(pltpu.VMEM((rows, 5 * DH), F32))
    return pl.pallas_call(
        functools.partial(attend_kernel, len(kvs), base, kind is not None),
        out_shape=shapes,
        scratch_shapes=scratch,
        compiler_params=PARAMS,
        cost_estimate=cost(rows, keys),
        name="attend",
    )(query, *kvs, state)


def join_kernel(mine, mine_stat, other, other_stat, keep, send, squares):
    yh = lax.axis_index("yh")
    half = keep.shape[0]
    for step, rows in enumerate((slice(0, half), slice(half, 2 * half))):
        top_a, top_b = mine_stat[rows, 0:1], other_stat[rows, 0:1]
        top = jnp.maximum(top_a, top_b)
        part_a, part_b = jnp.exp2(top_a - top), jnp.exp2(top_b - top)
        inverse = 1.0 / (part_a + part_b)
        part_a, part_b = part_a * inverse, part_b * inverse
        both = mine[rows, :] * part_a + other[rows, :].astype(F32) * part_b
        cross = mine_stat[rows, 1:2] * part_a + other_stat[rows, 1:2] * part_b
        out = both[:, :DH]
        moved = both[:, DH:] - cross * out
        kept = (keep, send)[step]
        kept[:, :DH] = out.astype(kept.dtype)
        kept[:, DH:] = moved.astype(kept.dtype)
        sums = lax.dot_general(
            jnp.ones((8, DH), F32),
            moved * moved,
            (((1,), (1,)), ((), ())),
            precision=lax.Precision.HIGHEST,
            preferred_element_type=F32,
        )
        row = lax.broadcasted_iota(jnp.int32, (8, DH), 0)
        slab = jnp.zeros((8, DH), F32)
        for i in range(half // DH):
            slab = jnp.where(row == i, sums[:, i * DH : (i + 1) * DH], slab)
        owner = yh if step == 0 else 1 - yh
        for i in range(8):
            squares[owner * 8 + i] = slab


def join(*arrays):
    half = arrays[0].shape[0] // 2
    return pl.pallas_call(
        join_kernel,
        out_shape=[
            jax.ShapeDtypeStruct((half, 2 * DH), F32),
            jax.ShapeDtypeStruct((half, 2 * DH), BF16),
            jax.ShapeDtypeStruct((16, 8, DH), F32),
        ],
        compiler_params=PARAMS,
        name="join",
    )(*arrays)


def finish_kernel(keep, come, squares, attended, unit):
    flip = lax.axis_index("yh") == 1
    sums = squares[0]
    for i in range(1, 16):
        sums = sums + squares[i]
    row = lax.broadcasted_iota(jnp.int32, (8, DH), 0)
    for i in range(keep.shape[0] // DH):
        rows = slice(i * DH, (i + 1) * DH)
        mean = lax.dot_general(
            jnp.where(row == i, sums, 0.0),
            jnp.full((8, DH), 1.0 / (HEADS * DH), F32),
            (((0,), (0,)), ((), ())),
            precision=lax.Precision.HIGHEST,
            preferred_element_type=F32,
        )
        inverse = 1.0 / jnp.sqrt(mean + 1e-06)
        mine, other = keep[rows, :DH].astype(BF16), come[rows, :DH]
        attended[rows, :DH] = jnp.where(flip, other, mine)
        attended[rows, DH:] = jnp.where(flip, mine, other)
        mine = (keep[rows, DH:] * inverse).astype(BF16)
        other = (come[rows, DH:].astype(F32) * inverse).astype(BF16)
        unit[rows, :DH] = jnp.where(flip, other, mine)
        unit[rows, DH:] = jnp.where(flip, mine, other)


def finish(*arrays):
    out = jax.ShapeDtypeStruct(arrays[1].shape, BF16)
    return pl.pallas_call(finish_kernel, out_shape=(out, out), compiler_params=PARAMS, name="finish")(*arrays)


def on_device(ring, q, k, v, qt, kt, vt):
    tokens = q.shape[0]
    hop_pairs = [(z * 2 + c, (z + 1 - 2 * c) % ring * 2 + c) for z in range(ring) for c in range(2)]
    hop = lambda a: lax.ppermute(a, ("z", "core"), hop_pairs)
    over_y = lambda a: lax.ppermute(a, "yh", SWAP)
    over_core = lambda a: lax.ppermute(a, "core", SWAP)
    def after(block, state):
        return lax.optimization_barrier((block, state))

    own_kv, own_q, other_kv, other_q = pack(q, k, v, qt, kt, vt)
    peer_kv = over_y(other_kv)
    other_q, peer_kv = after(other_q, peer_kv)
    peer_q = over_y(other_q)
    near = hop(jnp.concatenate([own_kv, over_core(own_kv)], axis=0))
    far = hop(jnp.concatenate([peer_kv, over_core(peer_kv)], axis=0))
    near_next = hop(near)
    pair_q = jnp.concatenate([own_q, peer_q], axis=0)
    state, query = begin(own_kv, peer_kv, pair_q, over_core(pair_q))
    near_two, state = after(near_next, state)
    near_next = hop(near_two)
    state = attend(query, [near], state)
    state = attend(query, [near_two], state)
    far, state = after(far, state)
    far_next = hop(far)
    state = attend(query, [far], state)
    near, state = after(near_next, state)
    part, state = after(near[:tokens], state)
    last_near = hop(part)
    state = attend(query, [near], state)
    far, state = after(far_next, state)
    far_next = hop(far)
    state = attend(query, [far], state)
    last_near, state = after(last_near, state)
    state = attend(query, [last_near], state)
    far, state = after(far_next, state)
    far_next = hop(far[:tokens])
    state = attend(query, [far], state)
    rows = query.shape[0]
    there, there_stat = attend(query, [far_next], state, (rows // 2, rows), BF16)
    come, come_stat = over_core(there), over_core(there_stat)
    here, here_stat = attend(query, [far_next], state, (0, rows // 2), F32)
    keep, send, squares = join(here, here_stat, come, come_stat)
    come = over_y(send)
    squares = lax.all_to_all(squares, ("yh", "yl", "x"), 0, 0, tiled=True)
    return finish(keep, come, squares)


def solution(mesh):
    fine = Mesh(mesh.devices.reshape(2, -1, 2, 2, mesh.shape["head"] // 2), ("yh", "z", "core", "yl", "x"))
    spec = P(("yh", "z", "core"), ("yl", "x"))
    return jax.shard_map(
        functools.partial(on_device, fine.shape["z"]),
        mesh=fine,
        in_specs=(spec,) * 6,
        out_specs=(spec, spec),
        check_vma=False,
    )
```

```python
import functools
import math

import jax
import jax.numpy as jnp
from jax import lax
from jax.experimental import pallas as pl
from jax.experimental.pallas import tpu as pltpu
from jax.sharding import Mesh
from jax.sharding import PartitionSpec as P

HEADS = 16
DH = 128
SCALE = 1.0 / math.sqrt(DH)
LOG2E = math.log2(math.e)
LIMIT = 2.0**40
TILE = 256
SMALL = 128
F32 = jnp.float32
BF16 = jnp.bfloat16
SWAP = ((0, 1), (1, 0))
PARAMS = pltpu.CompilerParams(vmem_limit_bytes=28 << 20)


def nt(a, b):
    return lax.dot_general(a, b, (((1,), (1,)), ((), ())), preferred_element_type=F32)


def nn(a, b):
    return lax.dot_general(a, b, (((1,), (0,)), ((), ())), preferred_element_type=F32)


def pack_kernel(q, k, v, qt, kt, vt, own_kv, own_q, other_kv, other_q):
    flip = lax.axis_index("yh") == 1
    spots = ((kt, 0, 0), (k, 0, 1), (v, 0, 2), (vt, 0, 3), (q, 1, 0), (qt, 1, 1))
    for ref, which, at in spots:
        low, high = ref[:, :DH], ref[:, DH:]
        cols = slice(at * DH, (at + 1) * DH)
        (own_kv, own_q)[which][:, cols] = jnp.where(flip, high, low)
        (other_kv, other_q)[which][:, cols] = jnp.where(flip, low, high)


def pack(*arrays):
    rows = arrays[0].shape[0]
    row = lambda width: pl.BlockSpec((rows // 2, width), lambda i: (i, 0))
    shapes = [jax.ShapeDtypeStruct((rows, n * DH), BF16) for n in (4, 2, 4, 2)]
    return pl.pallas_call(
        pack_kernel,
        grid=(2,),
        in_specs=[row(2 * DH)] * 6,
        out_specs=[row(n * DH) for n in (4, 2, 4, 2)],
        out_shape=shapes,
        compiler_params=pltpu.CompilerParams(vmem_limit_bytes=60 << 20),
        cost_estimate=pl.CostEstimate(flops=0, bytes_accessed=12 * rows * 2 * DH * 2, transcendentals=0),
        name="pack",
    )(*arrays)


def lanes(x):
    out = x[:, :DH]
    for i in range(1, x.shape[1] // DH):
        out = out + x[:, i * DH : (i + 1) * DH]
    return out


def wide(x, times):
    return jnp.concatenate([x] * times, axis=1)


def dots(query, kv):
    return nt(query[:, :DH], kv[:, DH : 2 * DH]), nt(query, kv[:, : 2 * DH])


def part(products, kv, old, exact):
    scores, tangent = products
    rows, keys = scores.shape
    scores = scores * (SCALE * LOG2E)
    if exact:
        top = jnp.broadcast_to(jnp.max(scores, axis=1, keepdims=True), (rows, DH))
        if old is not None:
            top = jnp.maximum(top, old[4])
    else:
        top = old[4]
    weights = jnp.exp2(scores - wide(top, keys // DH))
    tilted = weights * tangent
    total, cross = lanes(weights), lanes(tilted)
    both = nn(weights.astype(BF16), kv[:, 2 * DH :])
    moved = both[:, DH:] + nn(tilted.astype(BF16), kv[:, 2 * DH : 3 * DH]) * SCALE
    new = (both[:, :DH], moved, total, cross)
    if old is None:
        return (*new, top)
    if exact:
        factor = jnp.exp2(old[4] - top)
        return (*(n + o * factor for n, o in zip(new, old[:4])), top)
    return (*(n + o for n, o in zip(new, old[:4])), top)


def read(ref, rows):
    return tuple(ref[rows, i * DH : (i + 1) * DH] for i in range(5))


def write(ref, state, rows):
    for i, piece in enumerate(state):
        ref[rows, i * DH : (i + 1) * DH] = piece


def begin_kernel(own_kv, peer_kv, own_q, core_q, state, query, kv):
    rows = own_kv.shape[0]
    kv[:rows, :] = own_kv[...]
    kv[rows:, :] = peer_kv[...]
    query[: 2 * rows, :] = own_q[...]
    query[2 * rows :, :] = core_q[...]

    def body(i, carry):
        at = pl.multiple_of(i * 2 * TILE, 2 * TILE)
        spans = [pl.ds(at, TILE), pl.ds(at + TILE, TILE)]
        products = [dots(query[span, :], kv) for span in spans]
        for span, product in zip(spans, products):
            write(state, part(product, kv, None, True), span)
        return carry

    lax.fori_loop(0, query.shape[0] // (2 * TILE), body, 0)


def attend_kernel(blocks, base, last, q_ref, *refs):
    kv_refs = refs[:blocks]
    old_ref = refs[blocks]
    outs = refs[blocks + 1 : blocks + (3 if last else 2)]
    rest = list(refs[blocks + 1 + len(outs) :])
    kv = kv_refs[0]
    if blocks > 1:
        kv = rest.pop(0)
        at = 0
        for ref in kv_refs:
            kv[at : at + ref.shape[0], :] = ref[...]
            at += ref.shape[0]
    new_ref = rest.pop(0) if last else outs[0]
    rows, keys = new_ref.shape[0], kv.shape[0]
    each = 2 if rows % (2 * TILE) == 0 else rows // TILE

    def body(i, worst):
        starts = [pl.multiple_of(i * each * TILE, TILE) + n * TILE for n in range(each)]
        ahead = dots(q_ref[pl.ds(base + starts[0], TILE), :], kv)
        for n, at in enumerate(starts):
            now = ahead
            if n + 1 < each:
                ahead = dots(q_ref[pl.ds(base + starts[n + 1], TILE), :], kv)
            state = part(now, kv, read(old_ref, pl.ds(base + at, TILE)), False)
            write(new_ref, state, pl.ds(at, TILE))
            worst = jnp.maximum(worst, jnp.max(state[2].reshape(TILE // 8, 8, DH), axis=0))
        return worst

    worst = lax.fori_loop(0, rows // (each * TILE), body, jnp.zeros((8, DH), F32))

    @pl.when(jnp.logical_not(jnp.max(worst) < LIMIT))
    def _():
        def again(i, carry):
            at = pl.multiple_of(i * SMALL, SMALL)
            here, there = pl.ds(at, SMALL), pl.ds(base + at, SMALL)
            new_ref[here, :] = old_ref[there, :]

            def some(j, inner):
                block = kv[pl.ds(pl.multiple_of(j * 3 * DH, 3 * DH), 3 * DH), :]
                write(new_ref, part(dots(q_ref[there, :], block), block, read(new_ref, here), True), here)
                return inner

            return lax.fori_loop(0, keys // (3 * DH), some, carry)

        lax.fori_loop(0, rows // SMALL, again, 0)

    if last:
        out, stats = outs
        primal, moved, total, cross, top = read(new_ref, slice(0, rows))
        total = jnp.sum(total, axis=1, keepdims=True)
        cross = jnp.sum(cross, axis=1, keepdims=True)
        inverse = 1.0 / total
        out[:, :DH] = (primal * inverse).astype(out.dtype)
        out[:, DH:] = (moved * inverse).astype(out.dtype)
        lane = lax.broadcasted_iota(jnp.int32, top.shape, 1)
        stats[...] = jnp.where(lane == 0, top + jnp.log2(total), cross * (SCALE * inverse))


def cost():
    return pl.CostEstimate(flops=1024, bytes_accessed=1024, transcendentals=0)


def begin(*arrays):
    rows, keys = 4 * arrays[0].shape[0], 2 * arrays[0].shape[0]
    return pl.pallas_call(
        begin_kernel,
        out_shape=[jax.ShapeDtypeStruct((rows, 5 * DH), F32), jax.ShapeDtypeStruct((rows, 2 * DH), BF16)],
        scratch_shapes=[pltpu.VMEM((keys, 4 * DH), BF16)],
        compiler_params=PARAMS,
        cost_estimate=cost(),
        name="begin",
    )(*arrays)


def attend(query, kvs, state, span=None, kind=None):
    base, end = span or (0, query.shape[0])
    rows = end - base
    keys = sum(kv.shape[0] for kv in kvs)
    scratch = [pltpu.VMEM((keys, 4 * DH), BF16)] if len(kvs) > 1 else []
    if kind is None:
        shapes = jax.ShapeDtypeStruct((rows, 5 * DH), F32)
    else:
        shapes = [jax.ShapeDtypeStruct((rows, 2 * DH), kind), jax.ShapeDtypeStruct((rows, DH), F32)]
        scratch.append(pltpu.VMEM((rows, 5 * DH), F32))
    return pl.pallas_call(
        functools.partial(attend_kernel, len(kvs), base, kind is not None),
        out_shape=shapes,
        scratch_shapes=scratch,
        compiler_params=PARAMS,
        cost_estimate=cost(),
        name="attend",
    )(query, *kvs, state)


def join_kernel(mine, mine_stat, other, other_stat, keep, send, squares):
    yh = lax.axis_index("yh")
    half = keep.shape[0]
    for step, rows in enumerate((slice(0, half), slice(half, 2 * half))):
        top_a, top_b = mine_stat[rows, 0:1], other_stat[rows, 0:1]
        top = jnp.maximum(top_a, top_b)
        part_a, part_b = jnp.exp2(top_a - top), jnp.exp2(top_b - top)
        inverse = 1.0 / (part_a + part_b)
        part_a, part_b = part_a * inverse, part_b * inverse
        both = mine[rows, :] * part_a + other[rows, :].astype(F32) * part_b
        cross = mine_stat[rows, 1:2] * part_a + other_stat[rows, 1:2] * part_b
        out = both[:, :DH]
        moved = both[:, DH:] - cross * out
        kept = (keep, send)[step]
        kept[:, :DH] = out.astype(kept.dtype)
        kept[:, DH:] = moved.astype(kept.dtype)
        sums = lax.dot_general(
            jnp.ones((8, DH), F32),
            moved * moved,
            (((1,), (1,)), ((), ())),
            precision=lax.Precision.HIGHEST,
            preferred_element_type=F32,
        )
        row = lax.broadcasted_iota(jnp.int32, (8, DH), 0)
        slab = jnp.zeros((8, DH), F32)
        for i in range(half // DH):
            slab = jnp.where(row == i, sums[:, i * DH : (i + 1) * DH], slab)
        owner = yh if step == 0 else 1 - yh
        for i in range(8):
            squares[owner * 8 + i] = slab


def join(*arrays):
    half = arrays[0].shape[0] // 2
    return pl.pallas_call(
        join_kernel,
        out_shape=[
            jax.ShapeDtypeStruct((half, 2 * DH), F32),
            jax.ShapeDtypeStruct((half, 2 * DH), BF16),
            jax.ShapeDtypeStruct((16, 8, DH), F32),
        ],
        compiler_params=PARAMS,
        name="join",
    )(*arrays)


def finish_kernel(keep, come, squares, attended, unit):
    flip = lax.axis_index("yh") == 1
    sums = squares[0]
    for i in range(1, 16):
        sums = sums + squares[i]
    row = lax.broadcasted_iota(jnp.int32, (8, DH), 0)
    for i in range(keep.shape[0] // DH):
        rows = slice(i * DH, (i + 1) * DH)
        mean = lax.dot_general(
            jnp.where(row == i, sums, 0.0),
            jnp.full((8, DH), 1.0 / (HEADS * DH), F32),
            (((0,), (0,)), ((), ())),
            precision=lax.Precision.HIGHEST,
            preferred_element_type=F32,
        )
        inverse = 1.0 / jnp.sqrt(mean + 1e-06)
        mine, other = keep[rows, :DH].astype(BF16), come[rows, :DH]
        attended[rows, :DH] = jnp.where(flip, other, mine)
        attended[rows, DH:] = jnp.where(flip, mine, other)
        mine = (keep[rows, DH:] * inverse).astype(BF16)
        other = (come[rows, DH:].astype(F32) * inverse).astype(BF16)
        unit[rows, :DH] = jnp.where(flip, other, mine)
        unit[rows, DH:] = jnp.where(flip, mine, other)


def finish(*arrays):
    out = jax.ShapeDtypeStruct(arrays[1].shape, BF16)
    return pl.pallas_call(finish_kernel, out_shape=(out, out), compiler_params=PARAMS, name="finish")(*arrays)


def on_device(ring, q, k, v, qt, kt, vt):
    tokens = q.shape[0]
    hop_pairs = [(z * 2 + c, (z + 1 - 2 * c) % ring * 2 + c) for z in range(ring) for c in range(2)]
    hop = lambda a: lax.ppermute(a, ("z", "core"), hop_pairs)
    over_y = lambda a: lax.ppermute(a, "yh", SWAP)
    over_core = lambda a: lax.ppermute(a, "core", SWAP)
    def after(block, state):
        return lax.optimization_barrier((block, state))

    own_kv, own_q, other_kv, other_q = pack(q, k, v, qt, kt, vt)
    peer_q, peer_kv = over_y(other_q), over_y(other_kv)
    core_kv = over_core(own_kv)
    near = [hop(own_kv), hop(core_kv)]
    near[0], near[1], peer_kv, peer_q = lax.optimization_barrier((near[0], near[1], peer_kv, peer_q))
    far = [hop(peer_kv), hop(over_core(peer_kv))]
    near_next = [hop(a) for a in near]
    pair_q = jnp.concatenate([own_q, peer_q], axis=0)
    state, query = begin(own_kv, peer_kv, pair_q, over_core(pair_q))

    def turn(pair, state, count):
        sent, kept = [], []
        for i, block in enumerate(pair):
            block, state = after(block, state)
            kept.append(block)
            if i < count:
                sent.append(hop(block))
        return kept, sent, state

    near_two, near_three, state = turn(near_next, state, 2)
    state = attend(query, near, state)
    state = attend(query, near_two, state)
    far, far_next, state = turn(far, state, 2)
    state = attend(query, far, state)
    near, near_last, state = turn(near_three, state, 1)
    state = attend(query, near, state)
    far, far_next, state = turn(far_next, state, 2)
    state = attend(query, far, state)
    far, far_last, state = turn(far_next, state, 1)
    state = attend(query, near_last + far, state)
    far_next = far_last[0]
    rows = query.shape[0]
    there, there_stat = attend(query, [far_next], state, (rows // 2, rows), BF16)
    come, come_stat = over_core(there), over_core(there_stat)
    here, here_stat = attend(query, [far_next], state, (0, rows // 2), F32)
    keep, send, squares = join(here, here_stat, come, come_stat)
    come = over_y(send)
    squares = lax.all_to_all(squares, ("yh", "yl", "x"), 0, 0, tiled=True)
    return finish(keep, come, squares)


def solution(mesh):
    fine = Mesh(mesh.devices.reshape(2, -1, 2, 2, mesh.shape["head"] // 2), ("yh", "z", "core", "yl", "x"))
    spec = P(("yh", "z", "core"), ("yl", "x"))
    return jax.shard_map(
        functools.partial(on_device, fine.shape["z"]),
        mesh=fine,
        in_specs=(spec,) * 6,
        out_specs=(spec, spec),
        check_vma=False,
    )
```

```python
import functools
import math

import jax
import jax.numpy as jnp
from jax import lax
from jax.experimental import pallas as pl
from jax.experimental.pallas import tpu as pltpu
from jax.sharding import Mesh
from jax.sharding import PartitionSpec as P

HEADS = 16
DH = 128
SCALE = 1.0 / math.sqrt(DH)
LOG2E = math.log2(math.e)
LIMIT = 2.0**40
TILE = 256
SMALL = 128
F32 = jnp.float32
BF16 = jnp.bfloat16
SWAP = ((0, 1), (1, 0))
PARAMS = pltpu.CompilerParams(vmem_limit_bytes=28 << 20)


def nt(a, b):
    return lax.dot_general(a, b, (((1,), (1,)), ((), ())), preferred_element_type=F32)


def nn(a, b):
    return lax.dot_general(a, b, (((1,), (0,)), ((), ())), preferred_element_type=F32)


def pack_kernel(q, k, v, qt, kt, vt, own_kv, own_q, other_kv, other_q):
    flip = lax.axis_index("yh") == 1
    spots = ((kt, 0, 0), (k, 0, 1), (v, 0, 2), (vt, 0, 3), (q, 1, 0), (qt, 1, 1))
    for ref, which, at in spots:
        low, high = ref[:, :DH], ref[:, DH:]
        cols = slice(at * DH, (at + 1) * DH)
        (own_kv, own_q)[which][:, cols] = jnp.where(flip, high, low)
        (other_kv, other_q)[which][:, cols] = jnp.where(flip, low, high)


def pack(*arrays):
    rows = arrays[0].shape[0]
    row = lambda width: pl.BlockSpec((rows // 2, width), lambda i: (i, 0))
    shapes = [jax.ShapeDtypeStruct((rows, n * DH), BF16) for n in (4, 2, 4, 2)]
    return pl.pallas_call(
        pack_kernel,
        grid=(2,),
        in_specs=[row(2 * DH)] * 6,
        out_specs=[row(n * DH) for n in (4, 2, 4, 2)],
        out_shape=shapes,
        compiler_params=pltpu.CompilerParams(vmem_limit_bytes=60 << 20),
        cost_estimate=pl.CostEstimate(flops=0, bytes_accessed=12 * rows * 2 * DH * 2, transcendentals=0),
        name="pack",
    )(*arrays)


def lanes(x):
    out = x[:, :DH]
    for i in range(1, x.shape[1] // DH):
        out = out + x[:, i * DH : (i + 1) * DH]
    return out


def wide(x, times):
    return jnp.concatenate([x] * times, axis=1)


def dots(query, kv):
    return nt(query[:, :DH], kv[:, DH : 2 * DH]), nt(query, kv[:, : 2 * DH])


def part(products, kv, old, exact):
    scores, tangent = products
    rows, keys = scores.shape
    scores = scores * (SCALE * LOG2E)
    if exact:
        top = jnp.broadcast_to(jnp.max(scores, axis=1, keepdims=True), (rows, DH))
        if old is not None:
            top = jnp.maximum(top, old[4])
    else:
        top = old[4]
    weights = jnp.exp2(scores - wide(top, keys // DH))
    tilted = weights * tangent
    total, cross = lanes(weights), lanes(tilted)
    both = nn(weights.astype(BF16), kv[:, 2 * DH :])
    moved = both[:, DH:] + nn(tilted.astype(BF16), kv[:, 2 * DH : 3 * DH]) * SCALE
    new = (both[:, :DH], moved, total, cross)
    if old is None:
        return (*new, top)
    if exact:
        factor = jnp.exp2(old[4] - top)
        return (*(n + o * factor for n, o in zip(new, old[:4])), top)
    return (*(n + o for n, o in zip(new, old[:4])), top)


def read(ref, rows):
    return tuple(ref[rows, i * DH : (i + 1) * DH] for i in range(5))


def write(ref, state, rows):
    for i, piece in enumerate(state):
        ref[rows, i * DH : (i + 1) * DH] = piece


def begin_kernel(own_kv, peer_kv, own_q, core_q, state, query, kv):
    rows = own_kv.shape[0]
    kv[:rows, :] = own_kv[...]
    kv[rows:, :] = peer_kv[...]
    query[: 2 * rows, :] = own_q[...]
    query[2 * rows :, :] = core_q[...]

    def body(i, carry):
        at = pl.multiple_of(i * 2 * TILE, 2 * TILE)
        spans = [pl.ds(at, TILE), pl.ds(at + TILE, TILE)]
        products = [dots(query[span, :], kv) for span in spans]
        for span, product in zip(spans, products):
            write(state, part(product, kv, None, True), span)
        return carry

    lax.fori_loop(0, query.shape[0] // (2 * TILE), body, 0)


def attend_kernel(blocks, base, last, q_ref, *refs):
    kv_refs = refs[:blocks]
    old_ref = refs[blocks]
    outs = refs[blocks + 1 : blocks + (3 if last else 2)]
    rest = list(refs[blocks + 1 + len(outs) :])
    kv = kv_refs[0]
    if blocks > 1:
        kv = rest.pop(0)
        at = 0
        for ref in kv_refs:
            kv[at : at + ref.shape[0], :] = ref[...]
            at += ref.shape[0]
    new_ref = rest.pop(0) if last else outs[0]
    rows, keys = new_ref.shape[0], kv.shape[0]
    each = 2 if rows % (2 * TILE) == 0 else rows // TILE

    def body(i, worst):
        starts = [pl.multiple_of(i * each * TILE, TILE) + n * TILE for n in range(each)]
        ahead = dots(q_ref[pl.ds(base + starts[0], TILE), :], kv)
        for n, at in enumerate(starts):
            now = ahead
            if n + 1 < each:
                ahead = dots(q_ref[pl.ds(base + starts[n + 1], TILE), :], kv)
            state = part(now, kv, read(old_ref, pl.ds(base + at, TILE)), False)
            write(new_ref, state, pl.ds(at, TILE))
            worst = jnp.maximum(worst, jnp.max(state[2].reshape(TILE // 8, 8, DH), axis=0))
        return worst

    worst = lax.fori_loop(0, rows // (each * TILE), body, jnp.zeros((8, DH), F32))

    @pl.when(jnp.logical_not(jnp.max(worst) < LIMIT))
    def _():
        def again(i, carry):
            at = pl.multiple_of(i * SMALL, SMALL)
            here, there = pl.ds(at, SMALL), pl.ds(base + at, SMALL)
            new_ref[here, :] = old_ref[there, :]

            def some(j, inner):
                block = kv[pl.ds(pl.multiple_of(j * 3 * DH, 3 * DH), 3 * DH), :]
                write(new_ref, part(dots(q_ref[there, :], block), block, read(new_ref, here), True), here)
                return inner

            return lax.fori_loop(0, keys // (3 * DH), some, carry)

        lax.fori_loop(0, rows // SMALL, again, 0)

    if last:
        out, stats = outs
        primal, moved, total, cross, top = read(new_ref, slice(0, rows))
        total = jnp.sum(total, axis=1, keepdims=True)
        cross = jnp.sum(cross, axis=1, keepdims=True)
        inverse = 1.0 / total
        out[:, :DH] = (primal * inverse).astype(out.dtype)
        out[:, DH:] = (moved * inverse).astype(out.dtype)
        lane = lax.broadcasted_iota(jnp.int32, top.shape, 1)
        stats[...] = jnp.where(lane == 0, top + jnp.log2(total), cross * (SCALE * inverse))


def cost():
    return pl.CostEstimate(flops=1024, bytes_accessed=1024, transcendentals=0)


def begin(*arrays):
    rows, keys = 4 * arrays[0].shape[0], 2 * arrays[0].shape[0]
    return pl.pallas_call(
        begin_kernel,
        out_shape=[jax.ShapeDtypeStruct((rows, 5 * DH), F32), jax.ShapeDtypeStruct((rows, 2 * DH), BF16)],
        scratch_shapes=[pltpu.VMEM((keys, 4 * DH), BF16)],
        compiler_params=PARAMS,
        cost_estimate=cost(),
        name="begin",
    )(*arrays)


def attend(query, kvs, state, span=None, kind=None):
    base, end = span or (0, query.shape[0])
    rows = end - base
    keys = sum(kv.shape[0] for kv in kvs)
    scratch = [pltpu.VMEM((keys, 4 * DH), BF16)] if len(kvs) > 1 else []
    if kind is None:
        shapes = jax.ShapeDtypeStruct((rows, 5 * DH), F32)
    else:
        shapes = [jax.ShapeDtypeStruct((rows, 2 * DH), kind), jax.ShapeDtypeStruct((rows, DH), F32)]
        scratch.append(pltpu.VMEM((rows, 5 * DH), F32))
    return pl.pallas_call(
        functools.partial(attend_kernel, len(kvs), base, kind is not None),
        out_shape=shapes,
        scratch_shapes=scratch,
        compiler_params=PARAMS,
        cost_estimate=cost(),
        name="attend",
    )(query, *kvs, state)


def join_kernel(mine, mine_stat, other, other_stat, keep, send, squares):
    yh = lax.axis_index("yh")
    half = keep.shape[0]
    for step, rows in enumerate((slice(0, half), slice(half, 2 * half))):
        top_a, top_b = mine_stat[rows, 0:1], other_stat[rows, 0:1]
        top = jnp.maximum(top_a, top_b)
        part_a, part_b = jnp.exp2(top_a - top), jnp.exp2(top_b - top)
        inverse = 1.0 / (part_a + part_b)
        part_a, part_b = part_a * inverse, part_b * inverse
        both = mine[rows, :] * part_a + other[rows, :].astype(F32) * part_b
        cross = mine_stat[rows, 1:2] * part_a + other_stat[rows, 1:2] * part_b
        out = both[:, :DH]
        moved = both[:, DH:] - cross * out
        kept = (keep, send)[step]
        kept[:, :DH] = out.astype(kept.dtype)
        kept[:, DH:] = moved.astype(kept.dtype)
        sums = lax.dot_general(
            jnp.ones((8, DH), F32),
            moved * moved,
            (((1,), (1,)), ((), ())),
            precision=lax.Precision.HIGHEST,
            preferred_element_type=F32,
        )
        row = lax.broadcasted_iota(jnp.int32, (8, DH), 0)
        slab = jnp.zeros((8, DH), F32)
        for i in range(half // DH):
            slab = jnp.where(row == i, sums[:, i * DH : (i + 1) * DH], slab)
        owner = yh if step == 0 else 1 - yh
        for i in range(8):
            squares[owner * 8 + i] = slab


def join(*arrays):
    half = arrays[0].shape[0] // 2
    return pl.pallas_call(
        join_kernel,
        out_shape=[
            jax.ShapeDtypeStruct((half, 2 * DH), F32),
            jax.ShapeDtypeStruct((half, 2 * DH), BF16),
            jax.ShapeDtypeStruct((16, 8, DH), F32),
        ],
        compiler_params=PARAMS,
        name="join",
    )(*arrays)


def finish_kernel(keep, come, squares, attended, unit):
    flip = lax.axis_index("yh") == 1
    sums = squares[0]
    for i in range(1, 16):
        sums = sums + squares[i]
    row = lax.broadcasted_iota(jnp.int32, (8, DH), 0)
    for i in range(keep.shape[0] // DH):
        rows = slice(i * DH, (i + 1) * DH)
        mean = lax.dot_general(
            jnp.where(row == i, sums, 0.0),
            jnp.full((8, DH), 1.0 / (HEADS * DH), F32),
            (((0,), (0,)), ((), ())),
            precision=lax.Precision.HIGHEST,
            preferred_element_type=F32,
        )
        inverse = 1.0 / jnp.sqrt(mean + 1e-06)
        mine, other = keep[rows, :DH].astype(BF16), come[rows, :DH]
        attended[rows, :DH] = jnp.where(flip, other, mine)
        attended[rows, DH:] = jnp.where(flip, mine, other)
        mine = (keep[rows, DH:] * inverse).astype(BF16)
        other = (come[rows, DH:].astype(F32) * inverse).astype(BF16)
        unit[rows, :DH] = jnp.where(flip, other, mine)
        unit[rows, DH:] = jnp.where(flip, mine, other)


def finish(*arrays):
    out = jax.ShapeDtypeStruct(arrays[1].shape, BF16)
    return pl.pallas_call(finish_kernel, out_shape=(out, out), compiler_params=PARAMS, name="finish")(*arrays)


def on_device(ring, q, k, v, qt, kt, vt):
    tokens = q.shape[0]
    hop_pairs = [(z * 2 + c, (z + 1 - 2 * c) % ring * 2 + c) for z in range(ring) for c in range(2)]
    hop = lambda a: lax.ppermute(a, ("z", "core"), hop_pairs)
    over_y = lambda a: lax.ppermute(a, "yh", SWAP)
    over_core = lambda a: lax.ppermute(a, "core", SWAP)
    def after(block, state):
        return lax.optimization_barrier((block, state))

    own_kv, own_q, other_kv, other_q = pack(q, k, v, qt, kt, vt)
    peer_q, peer_kv = over_y(other_q), over_y(other_kv)
    core_kv = over_core(own_kv)
    near = [hop(own_kv), hop(core_kv)]
    near_next = [hop(a) for a in near]
    near_next[0], near_next[1], peer_kv, peer_q = lax.optimization_barrier((*near_next, peer_kv, peer_q))
    far = [hop(peer_kv), hop(over_core(peer_kv))]
    pair_q = jnp.concatenate([own_q, peer_q], axis=0)
    state, query = begin(own_kv, peer_kv, pair_q, over_core(pair_q))

    def turn(pair, state, count):
        sent, kept = [], []
        for i, block in enumerate(pair):
            block, state = after(block, state)
            kept.append(block)
            if i < count:
                sent.append(hop(block))
        return kept, sent, state

    near_two, near_three, state = turn(near_next, state, 2)
    state = attend(query, near, state)
    state = attend(query, near_two, state)
    far, far_next, state = turn(far, state, 2)
    state = attend(query, far, state)
    near, near_last, state = turn(near_three, state, 1)
    state = attend(query, near, state)
    far, far_next, state = turn(far_next, state, 2)
    state = attend(query, far, state)
    far, far_last, state = turn(far_next, state, 1)
    state = attend(query, far, state)
    ends = near_last + far_last
    rows = query.shape[0]
    there, there_stat = attend(query, ends, state, (rows // 2, rows), BF16)
    come, come_stat = over_core(there), over_core(there_stat)
    here, here_stat = attend(query, ends, state, (0, rows // 2), F32)
    keep, send, squares = join(here, here_stat, come, come_stat)
    come = over_y(send)
    squares = lax.all_to_all(squares, ("yh", "yl", "x"), 0, 0, tiled=True)
    return finish(keep, come, squares)


def solution(mesh):
    fine = Mesh(mesh.devices.reshape(2, -1, 2, 2, mesh.shape["head"] // 2), ("yh", "z", "core", "yl", "x"))
    spec = P(("yh", "z", "core"), ("yl", "x"))
    return jax.shard_map(
        functools.partial(on_device, fine.shape["z"]),
        mesh=fine,
        in_specs=(spec,) * 6,
        out_specs=(spec, spec),
        check_vma=False,
    )
```

```python
import functools
import math

import jax
import jax.numpy as jnp
from jax import lax
from jax.experimental import pallas as pl
from jax.experimental.pallas import tpu as pltpu
from jax.sharding import Mesh
from jax.sharding import PartitionSpec as P

HEADS = 16
DH = 128
SCALE = 1.0 / math.sqrt(DH)
LOG2E = math.log2(math.e)
LIMIT = 2.0**40
TILE = 256
SMALL = 128
F32 = jnp.float32
BF16 = jnp.bfloat16
SWAP = ((0, 1), (1, 0))
PARAMS = pltpu.CompilerParams(vmem_limit_bytes=28 << 20)


def nt(a, b):
    return lax.dot_general(a, b, (((1,), (1,)), ((), ())), preferred_element_type=F32)


def nn(a, b):
    return lax.dot_general(a, b, (((1,), (0,)), ((), ())), preferred_element_type=F32)


def pack_kernel(q, k, v, qt, kt, vt, own_kv, own_q, other):
    step = pl.program_id(0)
    flip = lax.axis_index("yh") == 1
    rows = q.shape[0]
    for at, ref in enumerate((kt, k, v, vt, q, qt)):
        low, high = ref[:, :DH], ref[:, DH:]
        mine, theirs = jnp.where(flip, high, low), jnp.where(flip, low, high)
        if at < 4:
            cols = slice(at * DH, (at + 1) * DH)
            own_kv[:, cols] = mine
            other[pl.ds(pl.multiple_of(step * rows, rows), rows), cols] = theirs
        else:
            own_q[:, (at - 4) * DH : (at - 3) * DH] = mine
            for half in range(2):

                @pl.when(step == half)
                def _():
                    first = (2 * half + at - 4) * DH
                    other[2 * rows :, first : first + DH] = theirs


def pack(*arrays):
    rows = arrays[0].shape[0]
    half = rows // 2
    row = lambda width: pl.BlockSpec((half, width), lambda i: (i, 0))
    return pl.pallas_call(
        pack_kernel,
        grid=(2,),
        in_specs=[row(2 * DH)] * 6,
        out_specs=[row(4 * DH), row(2 * DH), pl.BlockSpec((rows + half, 4 * DH), lambda i: (0, 0))],
        out_shape=[
            jax.ShapeDtypeStruct((rows, 4 * DH), BF16),
            jax.ShapeDtypeStruct((rows, 2 * DH), BF16),
            jax.ShapeDtypeStruct((rows + half, 4 * DH), BF16),
        ],
        compiler_params=pltpu.CompilerParams(vmem_limit_bytes=60 << 20),
        cost_estimate=pl.CostEstimate(flops=0, bytes_accessed=12 * rows * 2 * DH * 2, transcendentals=0),
        name="pack",
    )(*arrays)


def lanes(x):
    out = x[:, :DH]
    for i in range(1, x.shape[1] // DH):
        out = out + x[:, i * DH : (i + 1) * DH]
    return out


def wide(x, times):
    return jnp.concatenate([x] * times, axis=1)


def dots(query, kv):
    return nt(query[:, :DH], kv[:, DH : 2 * DH]), nt(query, kv[:, : 2 * DH])


def part(products, kv, old, exact):
    scores, tangent = products
    rows, keys = scores.shape
    scores = scores * (SCALE * LOG2E)
    if exact:
        top = jnp.broadcast_to(jnp.max(scores, axis=1, keepdims=True), (rows, DH))
        if old is not None:
            top = jnp.maximum(top, old[4])
    else:
        top = old[4]
    weights = jnp.exp2(scores - wide(top, keys // DH))
    tilted = weights * tangent
    total, cross = lanes(weights), lanes(tilted)
    both = nn(weights.astype(BF16), kv[:, 2 * DH :])
    moved = both[:, DH:] + nn(tilted.astype(BF16), kv[:, 2 * DH : 3 * DH]) * SCALE
    new = (both[:, :DH], moved, total, cross)
    if old is None:
        return (*new, top)
    if exact:
        factor = jnp.exp2(old[4] - top)
        return (*(n + o * factor for n, o in zip(new, old[:4])), top)
    return (*(n + o for n, o in zip(new, old[:4])), top)


def read(ref, rows):
    return tuple(ref[rows, i * DH : (i + 1) * DH] for i in range(5))


def write(ref, state, rows):
    for i, piece in enumerate(state):
        ref[rows, i * DH : (i + 1) * DH] = piece


def begin_kernel(own_kv, own_q, core_q, peer, peer_core, state, query, kv):
    rows = own_kv.shape[0]
    half = rows // 2
    kv[:rows, :] = own_kv[...]
    kv[rows:, :] = peer[:rows, :]
    query[:rows, :] = own_q[...]
    query[2 * rows : 3 * rows, :] = core_q[...]
    for at, ref in ((rows, peer), (3 * rows, peer_core)):
        query[at : at + half, :] = ref[rows:, : 2 * DH]
        query[at + half : at + rows, :] = ref[rows:, 2 * DH :]

    def body(i, carry):
        at = pl.multiple_of(i * 2 * TILE, 2 * TILE)
        spans = [pl.ds(at, TILE), pl.ds(at + TILE, TILE)]
        products = [dots(query[span, :], kv) for span in spans]
        for span, product in zip(spans, products):
            write(state, part(product, kv, None, True), span)
        return carry

    lax.fori_loop(0, query.shape[0] // (2 * TILE), body, 0)


def attend_kernel(blocks, base, last, q_ref, *refs):
    kv_refs = refs[:blocks]
    old_ref = refs[blocks]
    outs = refs[blocks + 1 : blocks + (3 if last else 2)]
    rest = list(refs[blocks + 1 + len(outs) :])
    kv = kv_refs[0]
    if blocks > 1:
        kv = rest.pop(0)
        at = 0
        for ref in kv_refs:
            kv[at : at + ref.shape[0], :] = ref[...]
            at += ref.shape[0]
    new_ref = rest.pop(0) if last else outs[0]
    rows, keys = new_ref.shape[0], kv.shape[0]
    each = 2 if rows % (2 * TILE) == 0 else rows // TILE

    def body(i, worst):
        starts = [pl.multiple_of(i * each * TILE, TILE) + n * TILE for n in range(each)]
        ahead = dots(q_ref[pl.ds(base + starts[0], TILE), :], kv)
        for n, at in enumerate(starts):
            now = ahead
            if n + 1 < each:
                ahead = dots(q_ref[pl.ds(base + starts[n + 1], TILE), :], kv)
            state = part(now, kv, read(old_ref, pl.ds(base + at, TILE)), False)
            write(new_ref, state, pl.ds(at, TILE))
            worst = jnp.maximum(worst, jnp.max(state[2].reshape(TILE // 8, 8, DH), axis=0))
        return worst

    worst = lax.fori_loop(0, rows // (each * TILE), body, jnp.zeros((8, DH), F32))

    @pl.when(jnp.logical_not(jnp.max(worst) < LIMIT))
    def _():
        def again(i, carry):
            at = pl.multiple_of(i * SMALL, SMALL)
            here, there = pl.ds(at, SMALL), pl.ds(base + at, SMALL)
            new_ref[here, :] = old_ref[there, :]

            def some(j, inner):
                block = kv[pl.ds(pl.multiple_of(j * 3 * DH, 3 * DH), 3 * DH), :]
                write(new_ref, part(dots(q_ref[there, :], block), block, read(new_ref, here), True), here)
                return inner

            return lax.fori_loop(0, keys // (3 * DH), some, carry)

        lax.fori_loop(0, rows // SMALL, again, 0)

    if last:
        out, stats = outs
        primal, moved, total, cross, top = read(new_ref, slice(0, rows))
        total = jnp.sum(total, axis=1, keepdims=True)
        cross = jnp.sum(cross, axis=1, keepdims=True)
        inverse = 1.0 / total
        out[:, :DH] = (primal * inverse).astype(out.dtype)
        out[:, DH:] = (moved * inverse).astype(out.dtype)
        lane = lax.broadcasted_iota(jnp.int32, top.shape, 1)
        stats[...] = jnp.where(lane == 0, top + jnp.log2(total), cross * (SCALE * inverse))


def cost():
    return pl.CostEstimate(flops=1024, bytes_accessed=1024, transcendentals=0)


def begin(*arrays):
    rows, keys = 4 * arrays[0].shape[0], 2 * arrays[0].shape[0]
    return pl.pallas_call(
        begin_kernel,
        out_shape=[jax.ShapeDtypeStruct((rows, 5 * DH), F32), jax.ShapeDtypeStruct((rows, 2 * DH), BF16)],
        scratch_shapes=[pltpu.VMEM((keys, 4 * DH), BF16)],
        compiler_params=PARAMS,
        cost_estimate=cost(),
        name="begin",
    )(*arrays)


def attend(query, kvs, state, span=None, kind=None):
    base, end = span or (0, query.shape[0])
    rows = end - base
    keys = sum(kv.shape[0] for kv in kvs)
    scratch = [pltpu.VMEM((keys, 4 * DH), BF16)] if len(kvs) > 1 else []
    if kind is None:
        shapes = jax.ShapeDtypeStruct((rows, 5 * DH), F32)
    else:
        shapes = [jax.ShapeDtypeStruct((rows, 2 * DH), kind), jax.ShapeDtypeStruct((rows, DH), F32)]
        scratch.append(pltpu.VMEM((rows, 5 * DH), F32))
    return pl.pallas_call(
        functools.partial(attend_kernel, len(kvs), base, kind is not None),
        out_shape=shapes,
        scratch_shapes=scratch,
        compiler_params=PARAMS,
        cost_estimate=cost(),
        name="attend",
    )(query, *kvs, state)


def join_kernel(mine, mine_stat, other, other_stat, keep, send, squares):
    yh = lax.axis_index("yh")
    half = keep.shape[0]
    for step, rows in enumerate((slice(0, half), slice(half, 2 * half))):
        top_a, top_b = mine_stat[rows, 0:1], other_stat[rows, 0:1]
        top = jnp.maximum(top_a, top_b)
        part_a, part_b = jnp.exp2(top_a - top), jnp.exp2(top_b - top)
        inverse = 1.0 / (part_a + part_b)
        part_a, part_b = part_a * inverse, part_b * inverse
        both = mine[rows, :] * part_a + other[rows, :].astype(F32) * part_b
        cross = mine_stat[rows, 1:2] * part_a + other_stat[rows, 1:2] * part_b
        out = both[:, :DH]
        moved = both[:, DH:] - cross * out
        kept = (keep, send)[step]
        kept[:, :DH] = out.astype(kept.dtype)
        kept[:, DH:] = moved.astype(kept.dtype)
        sums = lax.dot_general(
            jnp.ones((8, DH), F32),
            moved * moved,
            (((1,), (1,)), ((), ())),
            precision=lax.Precision.HIGHEST,
            preferred_element_type=F32,
        )
        row = lax.broadcasted_iota(jnp.int32, (8, DH), 0)
        slab = jnp.zeros((8, DH), F32)
        for i in range(half // DH):
            slab = jnp.where(row == i, sums[:, i * DH : (i + 1) * DH], slab)
        owner = yh if step == 0 else 1 - yh
        for i in range(8):
            squares[owner * 8 + i] = slab


def join(*arrays):
    half = arrays[0].shape[0] // 2
    return pl.pallas_call(
        join_kernel,
        out_shape=[
            jax.ShapeDtypeStruct((half, 2 * DH), F32),
            jax.ShapeDtypeStruct((half, 2 * DH), BF16),
            jax.ShapeDtypeStruct((16, 8, DH), F32),
        ],
        compiler_params=PARAMS,
        name="join",
    )(*arrays)


def finish_kernel(keep, come, squares, attended, unit):
    flip = lax.axis_index("yh") == 1
    sums = squares[0]
    for i in range(1, 16):
        sums = sums + squares[i]
    row = lax.broadcasted_iota(jnp.int32, (8, DH), 0)
    for i in range(keep.shape[0] // DH):
        rows = slice(i * DH, (i + 1) * DH)
        mean = lax.dot_general(
            jnp.where(row == i, sums, 0.0),
            jnp.full((8, DH), 1.0 / (HEADS * DH), F32),
            (((0,), (0,)), ((), ())),
            precision=lax.Precision.HIGHEST,
            preferred_element_type=F32,
        )
        inverse = 1.0 / jnp.sqrt(mean + 1e-06)
        mine, other = keep[rows, :DH].astype(BF16), come[rows, :DH]
        attended[rows, :DH] = jnp.where(flip, other, mine)
        attended[rows, DH:] = jnp.where(flip, mine, other)
        mine = (keep[rows, DH:] * inverse).astype(BF16)
        other = (come[rows, DH:].astype(F32) * inverse).astype(BF16)
        unit[rows, :DH] = jnp.where(flip, other, mine)
        unit[rows, DH:] = jnp.where(flip, mine, other)


def finish(*arrays):
    out = jax.ShapeDtypeStruct(arrays[1].shape, BF16)
    return pl.pallas_call(finish_kernel, out_shape=(out, out), compiler_params=PARAMS, name="finish")(*arrays)


def on_device(ring, q, k, v, qt, kt, vt):
    tokens = q.shape[0]
    hop_pairs = [(z * 2 + c, (z + 1 - 2 * c) % ring * 2 + c) for z in range(ring) for c in range(2)]
    hop = lambda a: lax.ppermute(a, ("z", "core"), hop_pairs)
    over_y = lambda a: lax.ppermute(a, "yh", SWAP)
    over_core = lambda a: lax.ppermute(a, "core", SWAP)
    def after(block, state):
        return lax.optimization_barrier((block, state))

    own_kv, own_q, other = pack(q, k, v, qt, kt, vt)
    peer = over_y(other)
    core_kv = over_core(own_kv)
    near = [hop(own_kv), hop(core_kv)]
    core_q = over_core(own_q)
    near_next = [hop(a) for a in near]
    near_next[0], near_next[1], peer, core_q = lax.optimization_barrier((*near_next, peer, core_q))
    peer_core = over_core(peer)
    far = [hop(peer[:tokens]), hop(peer_core[:tokens])]
    near_three = [hop(a) for a in near_next]
    state, query = begin(own_kv, own_q, core_q, peer, peer_core)

    def turn(pair, state, count):
        sent, kept = [], []
        for i, block in enumerate(pair):
            block, state = after(block, state)
            kept.append(block)
            if i < count:
                sent.append(hop(block))
        return kept, sent, state

    state = attend(query, near, state)
    state = attend(query, near_next, state)
    far, far_next, state = turn(far, state, 2)
    state = attend(query, far, state)
    near, near_last, state = turn(near_three, state, 1)
    state = attend(query, near, state)
    far, far_next, state = turn(far_next, state, 2)
    state = attend(query, far, state)
    far, far_last, state = turn(far_next, state, 1)
    state = attend(query, far, state)
    last_near, state = after(near_last[0], state)
    state = attend(query, [last_near], state)
    ends = far_last
    rows = query.shape[0]
    there, there_stat = attend(query, ends, state, (rows // 2, rows), BF16)
    come, come_stat = over_core(there), over_core(there_stat)
    here, here_stat = attend(query, ends, state, (0, rows // 2), F32)
    keep, send, squares = join(here, here_stat, come, come_stat)
    come = over_y(send)
    squares = lax.all_to_all(squares, ("yh", "yl", "x"), 0, 0, tiled=True)
    return finish(keep, come, squares)


def solution(mesh):
    fine = Mesh(mesh.devices.reshape(2, -1, 2, 2, mesh.shape["head"] // 2), ("yh", "z", "core", "yl", "x"))
    spec = P(("yh", "z", "core"), ("yl", "x"))
    return jax.shard_map(
        functools.partial(on_device, fine.shape["z"]),
        mesh=fine,
        in_specs=(spec,) * 6,
        out_specs=(spec, spec),
        check_vma=False,
    )
```

```python
import functools
import math

import jax
import jax.numpy as jnp
from jax import lax
from jax.experimental import pallas as pl
from jax.experimental.pallas import tpu as pltpu
from jax.sharding import Mesh
from jax.sharding import PartitionSpec as P

HEADS = 16
DH = 128
SCALE = 1.0 / math.sqrt(DH)
LOG2E = math.log2(math.e)
LIMIT = 2.0**40
TILE = 256
SMALL = 128
F32 = jnp.float32
BF16 = jnp.bfloat16
SWAP = ((0, 1), (1, 0))
PARAMS = pltpu.CompilerParams(vmem_limit_bytes=28 << 20)


def nt(a, b):
    return lax.dot_general(a, b, (((1,), (1,)), ((), ())), preferred_element_type=F32)


def nn(a, b):
    return lax.dot_general(a, b, (((1,), (0,)), ((), ())), preferred_element_type=F32)


def pack_kernel(q, k, v, qt, kt, vt, own_kv, own_q, other):
    step = pl.program_id(0)
    flip = lax.axis_index("yh") == 1
    rows = q.shape[0]
    for at, ref in enumerate((kt, k, v, vt, q, qt)):
        low, high = ref[:, :DH], ref[:, DH:]
        mine, theirs = jnp.where(flip, high, low), jnp.where(flip, low, high)
        if at < 4:
            cols = slice(at * DH, (at + 1) * DH)
            own_kv[:, cols] = mine
            other[pl.ds(pl.multiple_of(step * rows, rows), rows), cols] = theirs
        else:
            own_q[:, (at - 4) * DH : (at - 3) * DH] = mine
            for half in range(2):

                @pl.when(step == half)
                def _():
                    first = (2 * half + at - 4) * DH
                    other[2 * rows :, first : first + DH] = theirs


def pack(*arrays):
    rows = arrays[0].shape[0]
    half = rows // 2
    row = lambda width: pl.BlockSpec((half, width), lambda i: (i, 0))
    return pl.pallas_call(
        pack_kernel,
        grid=(2,),
        in_specs=[row(2 * DH)] * 6,
        out_specs=[row(4 * DH), row(2 * DH), pl.BlockSpec((rows + half, 4 * DH), lambda i: (0, 0))],
        out_shape=[
            jax.ShapeDtypeStruct((rows, 4 * DH), BF16),
            jax.ShapeDtypeStruct((rows, 2 * DH), BF16),
            jax.ShapeDtypeStruct((rows + half, 4 * DH), BF16),
        ],
        compiler_params=pltpu.CompilerParams(vmem_limit_bytes=60 << 20),
        cost_estimate=pl.CostEstimate(flops=0, bytes_accessed=12 * rows * 2 * DH * 2, transcendentals=0),
        name="pack",
    )(*arrays)


def lanes(x):
    out = x[:, :DH]
    for i in range(1, x.shape[1] // DH):
        out = out + x[:, i * DH : (i + 1) * DH]
    return out


def wide(x, times):
    return jnp.concatenate([x] * times, axis=1)


def dots(query, kv):
    return nt(query[:, :DH], kv[:, DH : 2 * DH]), nt(query, kv[:, : 2 * DH])


def part(products, kv, old, exact):
    scores, tangent = products
    rows, keys = scores.shape
    scores = scores * (SCALE * LOG2E)
    if exact:
        top = jnp.broadcast_to(jnp.max(scores, axis=1, keepdims=True), (rows, DH))
        if old is not None:
            top = jnp.maximum(top, old[4])
    else:
        top = old[4]
    weights = jnp.exp2(scores - wide(top, keys // DH))
    tilted = weights * tangent
    total, cross = lanes(weights), lanes(tilted)
    both = nn(weights.astype(BF16), kv[:, 2 * DH :])
    moved = both[:, DH:] + nn(tilted.astype(BF16), kv[:, 2 * DH : 3 * DH]) * SCALE
    new = (both[:, :DH], moved, total, cross)
    if old is None:
        return (*new, top)
    if exact:
        factor = jnp.exp2(old[4] - top)
        return (*(n + o * factor for n, o in zip(new, old[:4])), top)
    return (*(n + o for n, o in zip(new, old[:4])), top)


def read(ref, rows):
    return tuple(ref[rows, i * DH : (i + 1) * DH] for i in range(5))


def write(ref, state, rows):
    for i, piece in enumerate(state):
        ref[rows, i * DH : (i + 1) * DH] = piece


def begin_kernel(own_kv, own_q, core_q, peer, peer_core, state, query, kv):
    rows = own_kv.shape[0]
    half = rows // 2
    kv[:rows, :] = own_kv[...]
    kv[rows:, :] = peer[:rows, :]
    query[:rows, :] = own_q[...]
    query[2 * rows : 3 * rows, :] = core_q[...]
    for at, ref in ((rows, peer), (3 * rows, peer_core)):
        query[at : at + half, :] = ref[rows:, : 2 * DH]
        query[at + half : at + rows, :] = ref[rows:, 2 * DH :]

    def body(i, carry):
        at = pl.multiple_of(i * 2 * TILE, 2 * TILE)
        spans = [pl.ds(at, TILE), pl.ds(at + TILE, TILE)]
        products = [dots(query[span, :], kv) for span in spans]
        for span, product in zip(spans, products):
            write(state, part(product, kv, None, True), span)
        return carry

    lax.fori_loop(0, query.shape[0] // (2 * TILE), body, 0)


def attend_kernel(blocks, base, last, q_ref, *refs):
    kv_refs = refs[:blocks]
    old_ref = refs[blocks]
    outs = refs[blocks + 1 : blocks + (3 if last else 2)]
    rest = list(refs[blocks + 1 + len(outs) :])
    kv = kv_refs[0]
    if blocks > 1:
        kv = rest.pop(0)
        at = 0
        for ref in kv_refs:
            kv[at : at + ref.shape[0], :] = ref[...]
            at += ref.shape[0]
    new_ref = rest.pop(0) if last else outs[0]
    rows, keys = new_ref.shape[0], kv.shape[0]
    each = 2 if rows % (2 * TILE) == 0 else rows // TILE

    def body(i, worst):
        starts = [pl.multiple_of(i * each * TILE, TILE) + n * TILE for n in range(each)]
        ahead = dots(q_ref[pl.ds(base + starts[0], TILE), :], kv)
        for n, at in enumerate(starts):
            now = ahead
            if n + 1 < each:
                ahead = dots(q_ref[pl.ds(base + starts[n + 1], TILE), :], kv)
            state = part(now, kv, read(old_ref, pl.ds(base + at, TILE)), False)
            write(new_ref, state, pl.ds(at, TILE))
            worst = jnp.maximum(worst, jnp.max(state[2].reshape(TILE // 8, 8, DH), axis=0))
        return worst

    worst = lax.fori_loop(0, rows // (each * TILE), body, jnp.zeros((8, DH), F32))

    @pl.when(jnp.logical_not(jnp.max(worst) < LIMIT))
    def _():
        def again(i, carry):
            at = pl.multiple_of(i * SMALL, SMALL)
            here, there = pl.ds(at, SMALL), pl.ds(base + at, SMALL)
            new_ref[here, :] = old_ref[there, :]

            def some(j, inner):
                block = kv[pl.ds(pl.multiple_of(j * 3 * DH, 3 * DH), 3 * DH), :]
                write(new_ref, part(dots(q_ref[there, :], block), block, read(new_ref, here), True), here)
                return inner

            return lax.fori_loop(0, keys // (3 * DH), some, carry)

        lax.fori_loop(0, rows // SMALL, again, 0)

    if last:
        out, stats = outs
        primal, moved, total, cross, top = read(new_ref, slice(0, rows))
        total = jnp.sum(total, axis=1, keepdims=True)
        cross = jnp.sum(cross, axis=1, keepdims=True)
        inverse = 1.0 / total
        out[:, :DH] = (primal * inverse).astype(out.dtype)
        out[:, DH:] = (moved * inverse).astype(out.dtype)
        lane = lax.broadcasted_iota(jnp.int32, top.shape, 1)
        stats[...] = jnp.where(lane == 0, top + jnp.log2(total), cross * (SCALE * inverse))


def cost():
    return pl.CostEstimate(flops=1024, bytes_accessed=1024, transcendentals=0)


def begin(*arrays):
    rows, keys = 4 * arrays[0].shape[0], 2 * arrays[0].shape[0]
    return pl.pallas_call(
        begin_kernel,
        out_shape=[jax.ShapeDtypeStruct((rows, 5 * DH), F32), jax.ShapeDtypeStruct((rows, 2 * DH), BF16)],
        scratch_shapes=[pltpu.VMEM((keys, 4 * DH), BF16)],
        compiler_params=PARAMS,
        cost_estimate=cost(),
        name="begin",
    )(*arrays)


def attend(query, kvs, state, span=None, kind=None):
    base, end = span or (0, query.shape[0])
    rows = end - base
    keys = sum(kv.shape[0] for kv in kvs)
    scratch = [pltpu.VMEM((keys, 4 * DH), BF16)] if len(kvs) > 1 else []
    if kind is None:
        shapes = jax.ShapeDtypeStruct((rows, 5 * DH), F32)
    else:
        shapes = [jax.ShapeDtypeStruct((rows, 2 * DH), kind), jax.ShapeDtypeStruct((rows, DH), F32)]
        scratch.append(pltpu.VMEM((rows, 5 * DH), F32))
    return pl.pallas_call(
        functools.partial(attend_kernel, len(kvs), base, kind is not None),
        out_shape=shapes,
        scratch_shapes=scratch,
        compiler_params=PARAMS,
        cost_estimate=cost(),
        name="attend",
    )(query, *kvs, state)


def join_kernel(mine, mine_stat, other, other_stat, keep, send, squares):
    yh = lax.axis_index("yh")
    half = keep.shape[0]
    for step, rows in enumerate((slice(0, half), slice(half, 2 * half))):
        top_a, top_b = mine_stat[rows, 0:1], other_stat[rows, 0:1]
        top = jnp.maximum(top_a, top_b)
        part_a, part_b = jnp.exp2(top_a - top), jnp.exp2(top_b - top)
        inverse = 1.0 / (part_a + part_b)
        part_a, part_b = part_a * inverse, part_b * inverse
        both = mine[rows, :] * part_a + other[rows, :].astype(F32) * part_b
        cross = mine_stat[rows, 1:2] * part_a + other_stat[rows, 1:2] * part_b
        out = both[:, :DH]
        moved = both[:, DH:] - cross * out
        kept = (keep, send)[step]
        kept[:, :DH] = out.astype(kept.dtype)
        kept[:, DH:] = moved.astype(kept.dtype)
        sums = lax.dot_general(
            jnp.ones((8, DH), F32),
            moved * moved,
            (((1,), (1,)), ((), ())),
            precision=lax.Precision.HIGHEST,
            preferred_element_type=F32,
        )
        row = lax.broadcasted_iota(jnp.int32, (8, DH), 0)
        slab = jnp.zeros((8, DH), F32)
        for i in range(half // DH):
            slab = jnp.where(row == i, sums[:, i * DH : (i + 1) * DH], slab)
        owner = yh if step == 0 else 1 - yh
        for i in range(8):
            squares[owner * 8 + i] = slab


def join(*arrays):
    half = arrays[0].shape[0] // 2
    return pl.pallas_call(
        join_kernel,
        out_shape=[
            jax.ShapeDtypeStruct((half, 2 * DH), F32),
            jax.ShapeDtypeStruct((half, 2 * DH), BF16),
            jax.ShapeDtypeStruct((16, 8, DH), F32),
        ],
        compiler_params=PARAMS,
        name="join",
    )(*arrays)


def finish_kernel(keep, come, squares, attended, unit):
    flip = lax.axis_index("yh") == 1
    sums = squares[0]
    for i in range(1, 16):
        sums = sums + squares[i]
    row = lax.broadcasted_iota(jnp.int32, (8, DH), 0)
    for i in range(keep.shape[0] // DH):
        rows = slice(i * DH, (i + 1) * DH)
        mean = lax.dot_general(
            jnp.where(row == i, sums, 0.0),
            jnp.full((8, DH), 1.0 / (HEADS * DH), F32),
            (((0,), (0,)), ((), ())),
            precision=lax.Precision.HIGHEST,
            preferred_element_type=F32,
        )
        inverse = 1.0 / jnp.sqrt(mean + 1e-06)
        mine, other = keep[rows, :DH].astype(BF16), come[rows, :DH]
        attended[rows, :DH] = jnp.where(flip, other, mine)
        attended[rows, DH:] = jnp.where(flip, mine, other)
        mine = (keep[rows, DH:] * inverse).astype(BF16)
        other = (come[rows, DH:].astype(F32) * inverse).astype(BF16)
        unit[rows, :DH] = jnp.where(flip, other, mine)
        unit[rows, DH:] = jnp.where(flip, mine, other)


def finish(*arrays):
    out = jax.ShapeDtypeStruct(arrays[1].shape, BF16)
    return pl.pallas_call(finish_kernel, out_shape=(out, out), compiler_params=PARAMS, name="finish")(*arrays)


def on_device(ring, q, k, v, qt, kt, vt):
    tokens = q.shape[0]
    hop_pairs = [(z * 2 + c, (z + 1 - 2 * c) % ring * 2 + c) for z in range(ring) for c in range(2)]
    hop = lambda a: lax.ppermute(a, ("z", "core"), hop_pairs)
    over_y = lambda a: lax.ppermute(a, "yh", SWAP)
    over_core = lambda a: lax.ppermute(a, "core", SWAP)
    def after(block, state):
        return lax.optimization_barrier((block, state))

    own_kv, own_q, other = pack(q, k, v, qt, kt, vt)
    peer = over_y(other)
    core_kv = over_core(own_kv)
    near = [hop(own_kv), hop(core_kv)]
    core_q = over_core(own_q)
    near[0], core_q = after(near[0], core_q)
    near_next = [hop(a) for a in near]
    first, peer = after(near_next[0], peer)
    peer_core = over_core(peer)
    second, peer_kv = after(near_next[1], peer[:tokens])
    near_three = [hop(first), hop(second)]
    far = [hop(peer_kv), hop(peer_core[:tokens])]
    state, query = begin(own_kv, own_q, core_q, peer, peer_core)

    def turn(pair, state, count):
        sent, kept = [], []
        for i, block in enumerate(pair):
            block, state = after(block, state)
            kept.append(block)
            if i < count:
                sent.append(hop(block))
        return kept, sent, state

    state = attend(query, near, state)
    state = attend(query, near_next, state)
    far, far_next, state = turn(far, state, 2)
    state = attend(query, far, state)
    near, near_last, state = turn(near_three, state, 1)
    state = attend(query, near, state)
    far, far_next, state = turn(far_next, state, 2)
    state = attend(query, far, state)
    far, far_last, state = turn(far_next, state, 1)
    state = attend(query, far, state)
    last_near, state = after(near_last[0], state)
    state = attend(query, [last_near], state)
    ends = far_last
    rows = query.shape[0]
    there, there_stat = attend(query, ends, state, (rows // 2, rows), BF16)
    come, come_stat = over_core(there), over_core(there_stat)
    here, here_stat = attend(query, ends, state, (0, rows // 2), F32)
    keep, send, squares = join(here, here_stat, come, come_stat)
    come = over_y(send)
    squares = lax.all_to_all(squares, ("yh", "yl", "x"), 0, 0, tiled=True)
    return finish(keep, come, squares)


def solution(mesh):
    fine = Mesh(mesh.devices.reshape(2, -1, 2, 2, mesh.shape["head"] // 2), ("yh", "z", "core", "yl", "x"))
    spec = P(("yh", "z", "core"), ("yl", "x"))
    return jax.shard_map(
        functools.partial(on_device, fine.shape["z"]),
        mesh=fine,
        in_specs=(spec,) * 6,
        out_specs=(spec, spec),
        check_vma=False,
    )
```

```python
import functools
import math

import jax
import jax.numpy as jnp
from jax import lax
from jax.experimental import pallas as pl
from jax.experimental.pallas import tpu as pltpu
from jax.sharding import Mesh
from jax.sharding import PartitionSpec as P

HEADS = 16
DH = 128
SCALE = 1.0 / math.sqrt(DH)
LOG2E = math.log2(math.e)
LIMIT = 2.0**40
TILE = 256
SMALL = 128
F32 = jnp.float32
BF16 = jnp.bfloat16
SWAP = ((0, 1), (1, 0))
PARAMS = pltpu.CompilerParams(vmem_limit_bytes=28 << 20)


def nt(a, b):
    return lax.dot_general(a, b, (((1,), (1,)), ((), ())), preferred_element_type=F32)


def nn(a, b):
    return lax.dot_general(a, b, (((1,), (0,)), ((), ())), preferred_element_type=F32)


def pack_kernel(q, k, v, qt, kt, vt, own_kv, own_q, other):
    step = pl.program_id(0)
    flip = lax.axis_index("yh") == 1
    rows = q.shape[0]
    for at, ref in enumerate((kt, k, v, vt, q, qt)):
        low, high = ref[:, :DH], ref[:, DH:]
        mine, theirs = jnp.where(flip, high, low), jnp.where(flip, low, high)
        if at < 4:
            cols = slice(at * DH, (at + 1) * DH)
            own_kv[:, cols] = mine
            other[pl.ds(pl.multiple_of(step * rows, rows), rows), cols] = theirs
        else:
            own_q[:, (at - 4) * DH : (at - 3) * DH] = mine
            for half in range(2):

                @pl.when(step == half)
                def _():
                    first = (2 * half + at - 4) * DH
                    other[2 * rows :, first : first + DH] = theirs


def pack(*arrays):
    rows = arrays[0].shape[0]
    half = rows // 2
    row = lambda width: pl.BlockSpec((half, width), lambda i: (i, 0))
    return pl.pallas_call(
        pack_kernel,
        grid=(2,),
        in_specs=[row(2 * DH)] * 6,
        out_specs=[row(4 * DH), row(2 * DH), pl.BlockSpec((rows + half, 4 * DH), lambda i: (0, 0))],
        out_shape=[
            jax.ShapeDtypeStruct((rows, 4 * DH), BF16),
            jax.ShapeDtypeStruct((rows, 2 * DH), BF16),
            jax.ShapeDtypeStruct((rows + half, 4 * DH), BF16),
        ],
        compiler_params=pltpu.CompilerParams(vmem_limit_bytes=60 << 20),
        cost_estimate=pl.CostEstimate(flops=0, bytes_accessed=12 * rows * 2 * DH * 2, transcendentals=0),
        name="pack",
    )(*arrays)


def lanes(x):
    out = x[:, :DH]
    for i in range(1, x.shape[1] // DH):
        out = out + x[:, i * DH : (i + 1) * DH]
    return out


def wide(x, times):
    return jnp.concatenate([x] * times, axis=1)


def dots(query, kv):
    return nt(query[:, :DH], kv[:, DH : 2 * DH]), nt(query, kv[:, : 2 * DH])


def part(products, kv, old, exact):
    scores, tangent = products
    rows, keys = scores.shape
    scores = scores * (SCALE * LOG2E)
    if exact:
        top = jnp.broadcast_to(jnp.max(scores, axis=1, keepdims=True), (rows, DH))
        if old is not None:
            top = jnp.maximum(top, old[4])
    else:
        top = old[4]
    weights = jnp.exp2(scores - wide(top, keys // DH))
    tilted = weights * tangent
    total, cross = lanes(weights), lanes(tilted)
    both = nn(weights.astype(BF16), kv[:, 2 * DH :])
    moved = both[:, DH:] + nn(tilted.astype(BF16), kv[:, 2 * DH : 3 * DH]) * SCALE
    new = (both[:, :DH], moved, total, cross)
    if old is None:
        return (*new, top)
    if exact:
        factor = jnp.exp2(old[4] - top)
        return (*(n + o * factor for n, o in zip(new, old[:4])), top)
    return (*(n + o for n, o in zip(new, old[:4])), top)


def read(ref, rows):
    return tuple(ref[rows, i * DH : (i + 1) * DH] for i in range(5))


def write(ref, state, rows):
    for i, piece in enumerate(state):
        ref[rows, i * DH : (i + 1) * DH] = piece


def begin_kernel(own_kv, own_q, core_q, peer, peer_core, state, query, kv):
    rows = own_kv.shape[0]
    half = rows // 2
    kv[:rows, :] = own_kv[...]
    kv[rows:, :] = peer[:rows, :]
    query[:rows, :] = own_q[...]
    query[2 * rows : 3 * rows, :] = core_q[...]
    for at, ref in ((rows, peer), (3 * rows, peer_core)):
        query[at : at + half, :] = ref[rows:, : 2 * DH]
        query[at + half : at + rows, :] = ref[rows:, 2 * DH :]

    def body(i, carry):
        at = pl.multiple_of(i * 2 * TILE, 2 * TILE)
        spans = [pl.ds(at, TILE), pl.ds(at + TILE, TILE)]
        products = [dots(query[span, :], kv) for span in spans]
        for span, product in zip(spans, products):
            write(state, part(product, kv, None, True), span)
        return carry

    lax.fori_loop(0, query.shape[0] // (2 * TILE), body, 0)


def attend_kernel(blocks, base, last, q_ref, *refs):
    kv_refs = refs[:blocks]
    old_ref = refs[blocks]
    outs = refs[blocks + 1 : blocks + (3 if last else 2)]
    rest = list(refs[blocks + 1 + len(outs) :])
    kv = kv_refs[0]
    if blocks > 1:
        kv = rest.pop(0)
        at = 0
        for ref in kv_refs:
            kv[at : at + ref.shape[0], :] = ref[...]
            at += ref.shape[0]
    new_ref = rest.pop(0) if last else outs[0]
    rows, keys = new_ref.shape[0], kv.shape[0]
    each = 2 if rows % (2 * TILE) == 0 else rows // TILE

    def body(i, worst):
        starts = [pl.multiple_of(i * each * TILE, TILE) + n * TILE for n in range(each)]
        ahead = dots(q_ref[pl.ds(base + starts[0], TILE), :], kv)
        for n, at in enumerate(starts):
            now = ahead
            if n + 1 < each:
                ahead = dots(q_ref[pl.ds(base + starts[n + 1], TILE), :], kv)
            state = part(now, kv, read(old_ref, pl.ds(base + at, TILE)), False)
            write(new_ref, state, pl.ds(at, TILE))
            worst = jnp.maximum(worst, jnp.max(state[2].reshape(TILE // 8, 8, DH), axis=0))
        return worst

    worst = lax.fori_loop(0, rows // (each * TILE), body, jnp.zeros((8, DH), F32))

    @pl.when(jnp.logical_not(jnp.max(worst) < LIMIT))
    def _():
        def again(i, carry):
            at = pl.multiple_of(i * SMALL, SMALL)
            here, there = pl.ds(at, SMALL), pl.ds(base + at, SMALL)
            new_ref[here, :] = old_ref[there, :]

            def some(j, inner):
                block = kv[pl.ds(pl.multiple_of(j * 3 * DH, 3 * DH), 3 * DH), :]
                write(new_ref, part(dots(q_ref[there, :], block), block, read(new_ref, here), True), here)
                return inner

            return lax.fori_loop(0, keys // (3 * DH), some, carry)

        lax.fori_loop(0, rows // SMALL, again, 0)

    if last:
        out, stats = outs
        primal, moved, total, cross, top = read(new_ref, slice(0, rows))
        total = jnp.sum(total, axis=1, keepdims=True)
        cross = jnp.sum(cross, axis=1, keepdims=True)
        inverse = 1.0 / total
        out[:, :DH] = (primal * inverse).astype(out.dtype)
        out[:, DH:] = (moved * inverse).astype(out.dtype)
        lane = lax.broadcasted_iota(jnp.int32, top.shape, 1)
        stats[...] = jnp.where(lane == 0, top + jnp.log2(total), cross * (SCALE * inverse))


def cost():
    return pl.CostEstimate(flops=1024, bytes_accessed=1024, transcendentals=0)


def begin(*arrays):
    rows, keys = 4 * arrays[0].shape[0], 2 * arrays[0].shape[0]
    return pl.pallas_call(
        begin_kernel,
        out_shape=[jax.ShapeDtypeStruct((rows, 5 * DH), F32), jax.ShapeDtypeStruct((rows, 2 * DH), BF16)],
        scratch_shapes=[pltpu.VMEM((keys, 4 * DH), BF16)],
        compiler_params=PARAMS,
        cost_estimate=cost(),
        name="begin",
    )(*arrays)


def attend(query, kvs, state, span=None, kind=None):
    base, end = span or (0, query.shape[0])
    rows = end - base
    keys = sum(kv.shape[0] for kv in kvs)
    scratch = [pltpu.VMEM((keys, 4 * DH), BF16)] if len(kvs) > 1 else []
    if kind is None:
        shapes = jax.ShapeDtypeStruct((rows, 5 * DH), F32)
    else:
        shapes = [jax.ShapeDtypeStruct((rows, 2 * DH), kind), jax.ShapeDtypeStruct((rows, DH), F32)]
        scratch.append(pltpu.VMEM((rows, 5 * DH), F32))
    return pl.pallas_call(
        functools.partial(attend_kernel, len(kvs), base, kind is not None),
        out_shape=shapes,
        scratch_shapes=scratch,
        compiler_params=PARAMS,
        cost_estimate=cost(),
        name="attend",
    )(query, *kvs, state)


def join_kernel(mine, mine_stat, other, other_stat, keep, send, squares):
    yh = lax.axis_index("yh")
    half = keep.shape[0]
    for step, rows in enumerate((slice(0, half), slice(half, 2 * half))):
        top_a, top_b = mine_stat[rows, 0:1], other_stat[rows, 0:1]
        top = jnp.maximum(top_a, top_b)
        part_a, part_b = jnp.exp2(top_a - top), jnp.exp2(top_b - top)
        inverse = 1.0 / (part_a + part_b)
        part_a, part_b = part_a * inverse, part_b * inverse
        both = mine[rows, :] * part_a + other[rows, :].astype(F32) * part_b
        cross = mine_stat[rows, 1:2] * part_a + other_stat[rows, 1:2] * part_b
        out = both[:, :DH]
        moved = both[:, DH:] - cross * out
        kept = (keep, send)[step]
        kept[:, :DH] = out.astype(kept.dtype)
        kept[:, DH:] = moved.astype(kept.dtype)
        sums = lax.dot_general(
            jnp.ones((8, DH), F32),
            moved * moved,
            (((1,), (1,)), ((), ())),
            precision=lax.Precision.HIGHEST,
            preferred_element_type=F32,
        )
        row = lax.broadcasted_iota(jnp.int32, (8, DH), 0)
        slab = jnp.zeros((8, DH), F32)
        for i in range(half // DH):
            slab = jnp.where(row == i, sums[:, i * DH : (i + 1) * DH], slab)
        owner = yh if step == 0 else 1 - yh
        for i in range(8):
            squares[owner * 8 + i] = slab


def join(*arrays):
    half = arrays[0].shape[0] // 2
    return pl.pallas_call(
        join_kernel,
        out_shape=[
            jax.ShapeDtypeStruct((half, 2 * DH), F32),
            jax.ShapeDtypeStruct((half, 2 * DH), BF16),
            jax.ShapeDtypeStruct((16, 8, DH), F32),
        ],
        compiler_params=PARAMS,
        name="join",
    )(*arrays)


def finish_kernel(keep, come, squares, attended, unit):
    flip = lax.axis_index("yh") == 1
    sums = squares[0]
    for i in range(1, 16):
        sums = sums + squares[i]
    row = lax.broadcasted_iota(jnp.int32, (8, DH), 0)
    for i in range(keep.shape[0] // DH):
        rows = slice(i * DH, (i + 1) * DH)
        mean = lax.dot_general(
            jnp.where(row == i, sums, 0.0),
            jnp.full((8, DH), 1.0 / (HEADS * DH), F32),
            (((0,), (0,)), ((), ())),
            precision=lax.Precision.HIGHEST,
            preferred_element_type=F32,
        )
        inverse = 1.0 / jnp.sqrt(mean + 1e-06)
        mine, other = keep[rows, :DH].astype(BF16), come[rows, :DH]
        attended[rows, :DH] = jnp.where(flip, other, mine)
        attended[rows, DH:] = jnp.where(flip, mine, other)
        mine = (keep[rows, DH:] * inverse).astype(BF16)
        other = (come[rows, DH:].astype(F32) * inverse).astype(BF16)
        unit[rows, :DH] = jnp.where(flip, other, mine)
        unit[rows, DH:] = jnp.where(flip, mine, other)


def finish(*arrays):
    out = jax.ShapeDtypeStruct(arrays[1].shape, BF16)
    return pl.pallas_call(finish_kernel, out_shape=(out, out), compiler_params=PARAMS, name="finish")(*arrays)


def on_device(ring, q, k, v, qt, kt, vt):
    tokens = q.shape[0]
    hop_pairs = [(z * 2 + c, (z + 1 - 2 * c) % ring * 2 + c) for z in range(ring) for c in range(2)]
    hop = lambda a: lax.ppermute(a, ("z", "core"), hop_pairs)
    over_y = lambda a: lax.ppermute(a, "yh", SWAP)
    over_core = lambda a: lax.ppermute(a, "core", SWAP)
    def after(block, state):
        return lax.optimization_barrier((block, state))

    own_kv, own_q, other = pack(q, k, v, qt, kt, vt)
    peer = over_y(other)
    core_kv = over_core(own_kv)
    near = [hop(own_kv), hop(core_kv)]
    core_q = over_core(own_q)
    near[0], core_q = after(near[0], core_q)
    near_next = [hop(a) for a in near]
    near_three = [hop(a) for a in near_next]
    near_three[0], peer = after(near_three[0], peer)
    peer_core = over_core(peer)
    near_three[1], peer_kv = after(near_three[1], peer[:tokens])
    far = [hop(peer_kv), hop(peer_core[:tokens])]
    near_last = hop(near_three[0])
    state, query = begin(own_kv, own_q, core_q, peer, peer_core)

    def turn(pair, state, count):
        sent, kept = [], []
        for i, block in enumerate(pair):
            block, state = after(block, state)
            kept.append(block)
            if i < count:
                sent.append(hop(block))
        return kept, sent, state

    state = attend(query, near, state)
    far, far_two, state = turn(far, state, 2)
    state = attend(query, near_next, state)
    state = attend(query, near_three + [near_last], state)
    far_two, far_three, state = turn(far_two, state, 2)
    state = attend(query, far, state)
    state = attend(query, far_two, state)
    far_three, ends, state = turn(far_three, state, 1)
    state = attend(query, far_three, state)
    rows = query.shape[0]
    there, there_stat = attend(query, ends, state, (rows // 2, rows), BF16)
    come, come_stat = over_core(there), over_core(there_stat)
    here, here_stat = attend(query, ends, state, (0, rows // 2), F32)
    keep, send, squares = join(here, here_stat, come, come_stat)
    come = over_y(send)
    squares = lax.all_to_all(squares, ("yh", "yl", "x"), 0, 0, tiled=True)
    return finish(keep, come, squares)


def solution(mesh):
    fine = Mesh(mesh.devices.reshape(2, -1, 2, 2, mesh.shape["head"] // 2), ("yh", "z", "core", "yl", "x"))
    spec = P(("yh", "z", "core"), ("yl", "x"))
    return jax.shard_map(
        functools.partial(on_device, fine.shape["z"]),
        mesh=fine,
        in_specs=(spec,) * 6,
        out_specs=(spec, spec),
        check_vma=False,
    )
```

```python
import functools
import math

import jax
import jax.numpy as jnp
from jax import lax
from jax.experimental import pallas as pl
from jax.experimental.pallas import tpu as pltpu
from jax.sharding import Mesh
from jax.sharding import PartitionSpec as P

HEADS = 16
DH = 128
SCALE = 1.0 / math.sqrt(DH)
LOG2E = math.log2(math.e)
LIMIT = 2.0**40
TILE = 256
SMALL = 128
F32 = jnp.float32
BF16 = jnp.bfloat16
SWAP = ((0, 1), (1, 0))
PARAMS = pltpu.CompilerParams(vmem_limit_bytes=28 << 20)


def nt(a, b):
    return lax.dot_general(a, b, (((1,), (1,)), ((), ())), preferred_element_type=F32)


def nn(a, b):
    return lax.dot_general(a, b, (((1,), (0,)), ((), ())), preferred_element_type=F32)


def pack_kernel(q, k, v, qt, kt, vt, own_kv, own_q, other):
    step = pl.program_id(0)
    flip = lax.axis_index("yh") == 1
    rows = q.shape[0]
    for at, ref in enumerate((kt, k, v, vt, q, qt)):
        low, high = ref[:, :DH], ref[:, DH:]
        mine, theirs = jnp.where(flip, high, low), jnp.where(flip, low, high)
        if at < 4:
            cols = slice(at * DH, (at + 1) * DH)
            own_kv[:, cols] = mine
            other[pl.ds(pl.multiple_of(step * rows, rows), rows), cols] = theirs
        else:
            own_q[:, (at - 4) * DH : (at - 3) * DH] = mine
            for half in range(2):

                @pl.when(step == half)
                def _():
                    first = (2 * half + at - 4) * DH
                    other[2 * rows :, first : first + DH] = theirs


def pack(*arrays):
    rows = arrays[0].shape[0]
    half = rows // 2
    row = lambda width: pl.BlockSpec((half, width), lambda i: (i, 0))
    return pl.pallas_call(
        pack_kernel,
        grid=(2,),
        in_specs=[row(2 * DH)] * 6,
        out_specs=[row(4 * DH), row(2 * DH), pl.BlockSpec((rows + half, 4 * DH), lambda i: (0, 0))],
        out_shape=[
            jax.ShapeDtypeStruct((rows, 4 * DH), BF16),
            jax.ShapeDtypeStruct((rows, 2 * DH), BF16),
            jax.ShapeDtypeStruct((rows + half, 4 * DH), BF16),
        ],
        compiler_params=pltpu.CompilerParams(vmem_limit_bytes=60 << 20),
        cost_estimate=pl.CostEstimate(flops=0, bytes_accessed=12 * rows * 2 * DH * 2, transcendentals=0),
        name="pack",
    )(*arrays)


def lanes(x):
    out = x[:, :DH]
    for i in range(1, x.shape[1] // DH):
        out = out + x[:, i * DH : (i + 1) * DH]
    return out


def wide(x, times):
    return jnp.concatenate([x] * times, axis=1)


def dots(query, kv):
    return nt(query[:, :DH], kv[:, DH : 2 * DH]), nt(query, kv[:, : 2 * DH])


def part(products, kv, old, exact):
    scores, tangent = products
    rows, keys = scores.shape
    scores = scores * (SCALE * LOG2E)
    if exact:
        top = jnp.broadcast_to(jnp.max(scores, axis=1, keepdims=True), (rows, DH))
        if old is not None:
            top = jnp.maximum(top, old[4])
    else:
        top = old[4]
    weights = jnp.exp2(scores - wide(top, keys // DH))
    tilted = weights * tangent
    total, cross = lanes(weights), lanes(tilted)
    both = nn(weights.astype(BF16), kv[:, 2 * DH :])
    moved = both[:, DH:] + nn(tilted.astype(BF16), kv[:, 2 * DH : 3 * DH]) * SCALE
    new = (both[:, :DH], moved, total, cross)
    if old is None:
        return (*new, top)
    if exact:
        factor = jnp.exp2(old[4] - top)
        return (*(n + o * factor for n, o in zip(new, old[:4])), top)
    return (*(n + o for n, o in zip(new, old[:4])), top)


def read(ref, rows):
    return tuple(ref[rows, i * DH : (i + 1) * DH] for i in range(5))


def write(ref, state, rows):
    for i, piece in enumerate(state):
        ref[rows, i * DH : (i + 1) * DH] = piece


def begin_kernel(own_kv, own_q, core_q, peer, peer_core, state, query, kv):
    rows = own_kv.shape[0]
    half = rows // 2
    kv[:rows, :] = own_kv[...]
    kv[rows:, :] = peer[:rows, :]
    query[:rows, :] = own_q[...]
    query[2 * rows : 3 * rows, :] = core_q[...]
    for at, ref in ((rows, peer), (3 * rows, peer_core)):
        query[at : at + half, :] = ref[rows:, : 2 * DH]
        query[at + half : at + rows, :] = ref[rows:, 2 * DH :]

    def body(i, carry):
        at = pl.multiple_of(i * 2 * TILE, 2 * TILE)
        spans = [pl.ds(at, TILE), pl.ds(at + TILE, TILE)]
        products = [dots(query[span, :], kv) for span in spans]
        for span, product in zip(spans, products):
            write(state, part(product, kv, None, True), span)
        return carry

    lax.fori_loop(0, query.shape[0] // (2 * TILE), body, 0)


def attend_kernel(blocks, base, last, q_ref, *refs):
    kv_refs = refs[:blocks]
    old_ref = refs[blocks]
    outs = refs[blocks + 1 : blocks + (3 if last else 2)]
    rest = list(refs[blocks + 1 + len(outs) :])
    kv = kv_refs[0]
    if blocks > 1:
        kv = rest.pop(0)
        at = 0
        for ref in kv_refs:
            kv[at : at + ref.shape[0], :] = ref[...]
            at += ref.shape[0]
    new_ref = rest.pop(0) if last else outs[0]
    rows, keys = new_ref.shape[0], kv.shape[0]
    each = 2 if rows % (2 * TILE) == 0 else rows // TILE

    def body(i, worst):
        starts = [pl.multiple_of(i * each * TILE, TILE) + n * TILE for n in range(each)]
        ahead = dots(q_ref[pl.ds(base + starts[0], TILE), :], kv)
        for n, at in enumerate(starts):
            now = ahead
            if n + 1 < each:
                ahead = dots(q_ref[pl.ds(base + starts[n + 1], TILE), :], kv)
            state = part(now, kv, read(old_ref, pl.ds(base + at, TILE)), False)
            write(new_ref, state, pl.ds(at, TILE))
            worst = jnp.maximum(worst, jnp.max(state[2].reshape(TILE // 8, 8, DH), axis=0))
        return worst

    worst = lax.fori_loop(0, rows // (each * TILE), body, jnp.zeros((8, DH), F32))

    @pl.when(jnp.logical_not(jnp.max(worst) < LIMIT))
    def _():
        def again(i, carry):
            at = pl.multiple_of(i * SMALL, SMALL)
            here, there = pl.ds(at, SMALL), pl.ds(base + at, SMALL)
            new_ref[here, :] = old_ref[there, :]

            def some(j, inner):
                block = kv[pl.ds(pl.multiple_of(j * 3 * DH, 3 * DH), 3 * DH), :]
                write(new_ref, part(dots(q_ref[there, :], block), block, read(new_ref, here), True), here)
                return inner

            return lax.fori_loop(0, keys // (3 * DH), some, carry)

        lax.fori_loop(0, rows // SMALL, again, 0)

    if last:
        out, stats = outs
        primal, moved, total, cross, top = read(new_ref, slice(0, rows))
        total = jnp.sum(total, axis=1, keepdims=True)
        cross = jnp.sum(cross, axis=1, keepdims=True)
        inverse = 1.0 / total
        out[:, :DH] = (primal * inverse).astype(out.dtype)
        out[:, DH:] = (moved * inverse).astype(out.dtype)
        lane = lax.broadcasted_iota(jnp.int32, top.shape, 1)
        stats[...] = jnp.where(lane == 0, top + jnp.log2(total), cross * (SCALE * inverse))


def cost():
    return pl.CostEstimate(flops=1024, bytes_accessed=1024, transcendentals=0)


def begin(*arrays):
    rows, keys = 4 * arrays[0].shape[0], 2 * arrays[0].shape[0]
    return pl.pallas_call(
        begin_kernel,
        out_shape=[jax.ShapeDtypeStruct((rows, 5 * DH), F32), jax.ShapeDtypeStruct((rows, 2 * DH), BF16)],
        scratch_shapes=[pltpu.VMEM((keys, 4 * DH), BF16)],
        compiler_params=PARAMS,
        cost_estimate=cost(),
        name="begin",
    )(*arrays)


def attend(query, kvs, state, span=None, kind=None):
    base, end = span or (0, query.shape[0])
    rows = end - base
    keys = sum(kv.shape[0] for kv in kvs)
    scratch = [pltpu.VMEM((keys, 4 * DH), BF16)] if len(kvs) > 1 else []
    if kind is None:
        shapes = jax.ShapeDtypeStruct((rows, 5 * DH), F32)
    else:
        shapes = [jax.ShapeDtypeStruct((rows, 2 * DH), kind), jax.ShapeDtypeStruct((rows, DH), F32)]
        scratch.append(pltpu.VMEM((rows, 5 * DH), F32))
    return pl.pallas_call(
        functools.partial(attend_kernel, len(kvs), base, kind is not None),
        out_shape=shapes,
        scratch_shapes=scratch,
        compiler_params=PARAMS,
        cost_estimate=cost(),
        name="attend",
    )(query, *kvs, state)


def join_kernel(mine, mine_stat, other, other_stat, keep, send, squares):
    yh = lax.axis_index("yh")
    half = keep.shape[0]
    for step, rows in enumerate((slice(0, half), slice(half, 2 * half))):
        top_a, top_b = mine_stat[rows, 0:1], other_stat[rows, 0:1]
        top = jnp.maximum(top_a, top_b)
        part_a, part_b = jnp.exp2(top_a - top), jnp.exp2(top_b - top)
        inverse = 1.0 / (part_a + part_b)
        part_a, part_b = part_a * inverse, part_b * inverse
        both = mine[rows, :] * part_a + other[rows, :].astype(F32) * part_b
        cross = mine_stat[rows, 1:2] * part_a + other_stat[rows, 1:2] * part_b
        out = both[:, :DH]
        moved = both[:, DH:] - cross * out
        kept = (keep, send)[step]
        kept[:, :DH] = out.astype(kept.dtype)
        kept[:, DH:] = moved.astype(kept.dtype)
        sums = lax.dot_general(
            jnp.ones((8, DH), F32),
            moved * moved,
            (((1,), (1,)), ((), ())),
            precision=lax.Precision.HIGHEST,
            preferred_element_type=F32,
        )
        row = lax.broadcasted_iota(jnp.int32, (8, DH), 0)
        slab = jnp.zeros((8, DH), F32)
        for i in range(half // DH):
            slab = jnp.where(row == i, sums[:, i * DH : (i + 1) * DH], slab)
        owner = yh if step == 0 else 1 - yh
        for i in range(8):
            squares[owner * 8 + i] = slab


def join(*arrays):
    half = arrays[0].shape[0] // 2
    return pl.pallas_call(
        join_kernel,
        out_shape=[
            jax.ShapeDtypeStruct((half, 2 * DH), F32),
            jax.ShapeDtypeStruct((half, 2 * DH), BF16),
            jax.ShapeDtypeStruct((16, 8, DH), F32),
        ],
        compiler_params=PARAMS,
        name="join",
    )(*arrays)


def finish_kernel(keep, come, squares, attended, unit):
    flip = lax.axis_index("yh") == 1
    sums = squares[0]
    for i in range(1, 16):
        sums = sums + squares[i]
    row = lax.broadcasted_iota(jnp.int32, (8, DH), 0)
    for i in range(keep.shape[0] // DH):
        rows = slice(i * DH, (i + 1) * DH)
        mean = lax.dot_general(
            jnp.where(row == i, sums, 0.0),
            jnp.full((8, DH), 1.0 / (HEADS * DH), F32),
            (((0,), (0,)), ((), ())),
            precision=lax.Precision.HIGHEST,
            preferred_element_type=F32,
        )
        inverse = 1.0 / jnp.sqrt(mean + 1e-06)
        mine, other = keep[rows, :DH].astype(BF16), come[rows, :DH]
        attended[rows, :DH] = jnp.where(flip, other, mine)
        attended[rows, DH:] = jnp.where(flip, mine, other)
        mine = (keep[rows, DH:] * inverse).astype(BF16)
        other = (come[rows, DH:].astype(F32) * inverse).astype(BF16)
        unit[rows, :DH] = jnp.where(flip, other, mine)
        unit[rows, DH:] = jnp.where(flip, mine, other)


def finish(*arrays):
    out = jax.ShapeDtypeStruct(arrays[1].shape, BF16)
    return pl.pallas_call(finish_kernel, out_shape=(out, out), compiler_params=PARAMS, name="finish")(*arrays)


def on_device(ring, q, k, v, qt, kt, vt):
    tokens = q.shape[0]
    hop_pairs = [(z * 2 + c, (z + 1 - 2 * c) % ring * 2 + c) for z in range(ring) for c in range(2)]
    hop = lambda a: lax.ppermute(a, ("z", "core"), hop_pairs)
    over_y = lambda a: lax.ppermute(a, "yh", SWAP)
    over_core = lambda a: lax.ppermute(a, "core", SWAP)
    def after(block, state):
        return lax.optimization_barrier((block, state))

    own_kv, own_q, other = pack(q, k, v, qt, kt, vt)
    peer = over_y(other)
    core_kv = over_core(own_kv)
    near = [hop(own_kv), hop(core_kv)]
    near_next = [hop(a) for a in near]
    first, peer = after(near_next[0], peer)
    peer_core = over_core(peer)
    second, peer_kv = after(near_next[1], peer[:tokens])
    near_three = [hop(first), hop(second)]
    far = [hop(peer_kv), hop(peer_core[:tokens])]
    core_q = over_core(own_q)
    state, query = begin(own_kv, own_q, core_q, peer, peer_core)

    def turn(pair, state, count):
        sent, kept = [], []
        for i, block in enumerate(pair):
            block, state = after(block, state)
            kept.append(block)
            if i < count:
                sent.append(hop(block))
        return kept, sent, state

    state = attend(query, near, state)
    state = attend(query, near_next, state)
    far, far_next, state = turn(far, state, 2)
    state = attend(query, far, state)
    near, near_last, state = turn(near_three, state, 1)
    state = attend(query, near, state)
    far, far_next, state = turn(far_next, state, 2)
    state = attend(query, far, state)
    far, far_last, state = turn(far_next, state, 1)
    state = attend(query, far, state)
    last_near, state = after(near_last[0], state)
    state = attend(query, [last_near], state)
    ends = far_last
    rows = query.shape[0]
    there, there_stat = attend(query, ends, state, (rows // 2, rows), BF16)
    come, come_stat = over_core(there), over_core(there_stat)
    here, here_stat = attend(query, ends, state, (0, rows // 2), F32)
    keep, send, squares = join(here, here_stat, come, come_stat)
    come = over_y(send)
    squares = lax.all_to_all(squares, ("yh", "yl", "x"), 0, 0, tiled=True)
    return finish(keep, come, squares)


def solution(mesh):
    fine = Mesh(mesh.devices.reshape(2, -1, 2, 2, mesh.shape["head"] // 2), ("yh", "z", "core", "yl", "x"))
    spec = P(("yh", "z", "core"), ("yl", "x"))
    return jax.shard_map(
        functools.partial(on_device, fine.shape["z"]),
        mesh=fine,
        in_specs=(spec,) * 6,
        out_specs=(spec, spec),
        check_vma=False,
    )
```

```python
import functools
import math

import jax
import jax.numpy as jnp
from jax import lax
from jax.experimental import pallas as pl
from jax.experimental.pallas import tpu as pltpu
from jax.sharding import Mesh
from jax.sharding import PartitionSpec as P

HEADS = 16
DH = 128
SCALE = 1.0 / math.sqrt(DH)
LOG2E = math.log2(math.e)
LIMIT = 2.0**40
TILE = 256
SMALL = 128
F32 = jnp.float32
BF16 = jnp.bfloat16
SWAP = ((0, 1), (1, 0))
PARAMS = pltpu.CompilerParams(vmem_limit_bytes=28 << 20)


def nt(a, b):
    return lax.dot_general(a, b, (((1,), (1,)), ((), ())), preferred_element_type=F32)


def nn(a, b):
    return lax.dot_general(a, b, (((1,), (0,)), ((), ())), preferred_element_type=F32)


def pack_kernel(q, k, v, qt, kt, vt, own_kv, own_q, other):
    step = pl.program_id(0)
    flip = lax.axis_index("yh") == 1
    rows = q.shape[0]
    for at, ref in enumerate((kt, k, v, vt, q, qt)):
        low, high = ref[:, :DH], ref[:, DH:]
        mine, theirs = jnp.where(flip, high, low), jnp.where(flip, low, high)
        if at < 4:
            cols = slice(at * DH, (at + 1) * DH)
            own_kv[:, cols] = mine
            other[pl.ds(pl.multiple_of(step * rows, rows), rows), cols] = theirs
        else:
            own_q[:, (at - 4) * DH : (at - 3) * DH] = mine
            for half in range(2):

                @pl.when(step == half)
                def _():
                    first = (2 * half + at - 4) * DH
                    other[2 * rows :, first : first + DH] = theirs


def pack(*arrays):
    rows = arrays[0].shape[0]
    half = rows // 2
    row = lambda width: pl.BlockSpec((half, width), lambda i: (i, 0))
    return pl.pallas_call(
        pack_kernel,
        grid=(2,),
        in_specs=[row(2 * DH)] * 6,
        out_specs=[row(4 * DH), row(2 * DH), pl.BlockSpec((rows + half, 4 * DH), lambda i: (0, 0))],
        out_shape=[
            jax.ShapeDtypeStruct((rows, 4 * DH), BF16),
            jax.ShapeDtypeStruct((rows, 2 * DH), BF16),
            jax.ShapeDtypeStruct((rows + half, 4 * DH), BF16),
        ],
        compiler_params=pltpu.CompilerParams(vmem_limit_bytes=60 << 20),
        cost_estimate=pl.CostEstimate(flops=0, bytes_accessed=12 * rows * 2 * DH * 2, transcendentals=0),
        name="pack",
    )(*arrays)


def lanes(x):
    out = x[:, :DH]
    for i in range(1, x.shape[1] // DH):
        out = out + x[:, i * DH : (i + 1) * DH]
    return out


def wide(x, times):
    return jnp.concatenate([x] * times, axis=1)


def dots(query, kv):
    return nt(query[:, :DH], kv[:, DH : 2 * DH]), nt(query, kv[:, : 2 * DH])


def part(products, kv, old, exact):
    scores, tangent = products
    rows, keys = scores.shape
    scores = scores * (SCALE * LOG2E)
    if exact:
        top = jnp.broadcast_to(jnp.max(scores, axis=1, keepdims=True), (rows, DH))
        if old is not None:
            top = jnp.maximum(top, old[4])
    else:
        top = old[4]
    weights = jnp.exp2(scores - wide(top, keys // DH))
    tilted = weights * tangent
    total, cross = lanes(weights), lanes(tilted)
    both = nn(weights.astype(BF16), kv[:, 2 * DH :])
    moved = both[:, DH:] + nn(tilted.astype(BF16), kv[:, 2 * DH : 3 * DH]) * SCALE
    new = (both[:, :DH], moved, total, cross)
    if old is None:
        return (*new, top)
    if exact:
        factor = jnp.exp2(old[4] - top)
        return (*(n + o * factor for n, o in zip(new, old[:4])), top)
    return (*(n + o for n, o in zip(new, old[:4])), top)


def read(ref, rows):
    return tuple(ref[rows, i * DH : (i + 1) * DH] for i in range(5))


def write(ref, state, rows):
    for i, piece in enumerate(state):
        ref[rows, i * DH : (i + 1) * DH] = piece


def begin_kernel(own_kv, own_q, core_q, peer, peer_core, state, query, kv):
    rows = own_kv.shape[0]
    half = rows // 2
    kv[:rows, :] = own_kv[...]
    kv[rows:, :] = peer[:rows, :]
    query[:rows, :] = own_q[...]
    query[2 * rows : 3 * rows, :] = core_q[...]
    for at, ref in ((rows, peer), (3 * rows, peer_core)):
        query[at : at + half, :] = ref[rows:, : 2 * DH]
        query[at + half : at + rows, :] = ref[rows:, 2 * DH :]

    def body(i, carry):
        at = pl.multiple_of(i * 2 * TILE, 2 * TILE)
        spans = [pl.ds(at, TILE), pl.ds(at + TILE, TILE)]
        products = [dots(query[span, :], kv) for span in spans]
        for span, product in zip(spans, products):
            write(state, part(product, kv, None, True), span)
        return carry

    lax.fori_loop(0, query.shape[0] // (2 * TILE), body, 0)


def attend_kernel(blocks, base, last, q_ref, *refs):
    kv_refs = refs[:blocks]
    old_ref = refs[blocks]
    outs = refs[blocks + 1 : blocks + (3 if last else 2)]
    rest = list(refs[blocks + 1 + len(outs) :])
    kv = kv_refs[0]
    if blocks > 1:
        kv = rest.pop(0)
        at = 0
        for ref in kv_refs:
            kv[at : at + ref.shape[0], :] = ref[...]
            at += ref.shape[0]
    new_ref = rest.pop(0) if last else outs[0]
    rows, keys = new_ref.shape[0], kv.shape[0]
    each = 2 if rows % (2 * TILE) == 0 else rows // TILE

    def body(i, worst):
        starts = [pl.multiple_of(i * each * TILE, TILE) + n * TILE for n in range(each)]
        ahead = dots(q_ref[pl.ds(base + starts[0], TILE), :], kv)
        for n, at in enumerate(starts):
            now = ahead
            if n + 1 < each:
                ahead = dots(q_ref[pl.ds(base + starts[n + 1], TILE), :], kv)
            state = part(now, kv, read(old_ref, pl.ds(base + at, TILE)), False)
            write(new_ref, state, pl.ds(at, TILE))
            worst = jnp.maximum(worst, jnp.max(state[2].reshape(TILE // 8, 8, DH), axis=0))
        return worst

    worst = lax.fori_loop(0, rows // (each * TILE), body, jnp.zeros((8, DH), F32))

    @pl.when(jnp.logical_not(jnp.max(worst) < LIMIT))
    def _():
        def again(i, carry):
            at = pl.multiple_of(i * SMALL, SMALL)
            here, there = pl.ds(at, SMALL), pl.ds(base + at, SMALL)
            new_ref[here, :] = old_ref[there, :]

            def some(j, inner):
                block = kv[pl.ds(pl.multiple_of(j * 3 * DH, 3 * DH), 3 * DH), :]
                write(new_ref, part(dots(q_ref[there, :], block), block, read(new_ref, here), True), here)
                return inner

            return lax.fori_loop(0, keys // (3 * DH), some, carry)

        lax.fori_loop(0, rows // SMALL, again, 0)

    if last:
        out, stats = outs
        primal, moved, total, cross, top = read(new_ref, slice(0, rows))
        total = jnp.sum(total, axis=1, keepdims=True)
        cross = jnp.sum(cross, axis=1, keepdims=True)
        inverse = 1.0 / total
        out[:, :DH] = (primal * inverse).astype(out.dtype)
        out[:, DH:] = (moved * inverse).astype(out.dtype)
        lane = lax.broadcasted_iota(jnp.int32, top.shape, 1)
        stats[...] = jnp.where(lane == 0, top + jnp.log2(total), cross * (SCALE * inverse))


def cost():
    return pl.CostEstimate(flops=1024, bytes_accessed=1024, transcendentals=0)


def begin(*arrays):
    rows, keys = 4 * arrays[0].shape[0], 2 * arrays[0].shape[0]
    return pl.pallas_call(
        begin_kernel,
        out_shape=[jax.ShapeDtypeStruct((rows, 5 * DH), F32), jax.ShapeDtypeStruct((rows, 2 * DH), BF16)],
        scratch_shapes=[pltpu.VMEM((keys, 4 * DH), BF16)],
        compiler_params=PARAMS,
        cost_estimate=cost(),
        name="begin",
    )(*arrays)


def attend(query, kvs, state, span=None, kind=None):
    base, end = span or (0, query.shape[0])
    rows = end - base
    keys = sum(kv.shape[0] for kv in kvs)
    scratch = [pltpu.VMEM((keys, 4 * DH), BF16)] if len(kvs) > 1 else []
    if kind is None:
        shapes = jax.ShapeDtypeStruct((rows, 5 * DH), F32)
    else:
        shapes = [jax.ShapeDtypeStruct((rows, 2 * DH), kind), jax.ShapeDtypeStruct((rows, DH), F32)]
        scratch.append(pltpu.VMEM((rows, 5 * DH), F32))
    return pl.pallas_call(
        functools.partial(attend_kernel, len(kvs), base, kind is not None),
        out_shape=shapes,
        scratch_shapes=scratch,
        compiler_params=PARAMS,
        cost_estimate=cost(),
        name="attend",
    )(query, *kvs, state)


def join_kernel(mine, mine_stat, other, other_stat, keep, send, squares):
    yh = lax.axis_index("yh")
    half = keep.shape[0]
    for step, rows in enumerate((slice(0, half), slice(half, 2 * half))):
        top_a, top_b = mine_stat[rows, 0:1], other_stat[rows, 0:1]
        top = jnp.maximum(top_a, top_b)
        part_a, part_b = jnp.exp2(top_a - top), jnp.exp2(top_b - top)
        inverse = 1.0 / (part_a + part_b)
        part_a, part_b = part_a * inverse, part_b * inverse
        both = mine[rows, :] * part_a + other[rows, :].astype(F32) * part_b
        cross = mine_stat[rows, 1:2] * part_a + other_stat[rows, 1:2] * part_b
        out = both[:, :DH]
        moved = both[:, DH:] - cross * out
        kept = (keep, send)[step]
        kept[:, :DH] = out.astype(kept.dtype)
        kept[:, DH:] = moved.astype(kept.dtype)
        sums = lax.dot_general(
            jnp.ones((8, DH), F32),
            moved * moved,
            (((1,), (1,)), ((), ())),
            precision=lax.Precision.HIGHEST,
            preferred_element_type=F32,
        )
        row = lax.broadcasted_iota(jnp.int32, (8, DH), 0)
        slab = jnp.zeros((8, DH), F32)
        for i in range(half // DH):
            slab = jnp.where(row == i, sums[:, i * DH : (i + 1) * DH], slab)
        owner = yh if step == 0 else 1 - yh
        for i in range(8):
            squares[owner * 8 + i] = slab


def join(*arrays):
    half = arrays[0].shape[0] // 2
    return pl.pallas_call(
        join_kernel,
        out_shape=[
            jax.ShapeDtypeStruct((half, 2 * DH), F32),
            jax.ShapeDtypeStruct((half, 2 * DH), BF16),
            jax.ShapeDtypeStruct((16, 8, DH), F32),
        ],
        compiler_params=PARAMS,
        name="join",
    )(*arrays)


def finish_kernel(keep, come, squares, attended, unit):
    flip = lax.axis_index("yh") == 1
    sums = squares[0]
    for i in range(1, 16):
        sums = sums + squares[i]
    row = lax.broadcasted_iota(jnp.int32, (8, DH), 0)
    for i in range(keep.shape[0] // DH):
        rows = slice(i * DH, (i + 1) * DH)
        mean = lax.dot_general(
            jnp.where(row == i, sums, 0.0),
            jnp.full((8, DH), 1.0 / (HEADS * DH), F32),
            (((0,), (0,)), ((), ())),
            precision=lax.Precision.HIGHEST,
            preferred_element_type=F32,
        )
        inverse = 1.0 / jnp.sqrt(mean + 1e-06)
        mine, other = keep[rows, :DH].astype(BF16), come[rows, :DH]
        attended[rows, :DH] = jnp.where(flip, other, mine)
        attended[rows, DH:] = jnp.where(flip, mine, other)
        mine = (keep[rows, DH:] * inverse).astype(BF16)
        other = (come[rows, DH:].astype(F32) * inverse).astype(BF16)
        unit[rows, :DH] = jnp.where(flip, other, mine)
        unit[rows, DH:] = jnp.where(flip, mine, other)


def finish(*arrays):
    out = jax.ShapeDtypeStruct(arrays[1].shape, BF16)
    return pl.pallas_call(finish_kernel, out_shape=(out, out), compiler_params=PARAMS, name="finish")(*arrays)


def on_device(ring, q, k, v, qt, kt, vt):
    tokens = q.shape[0]
    hop_pairs = [(z * 2 + c, (z + 1 - 2 * c) % ring * 2 + c) for z in range(ring) for c in range(2)]
    hop = lambda a: lax.ppermute(a, ("z", "core"), hop_pairs)
    over_y = lambda a: lax.ppermute(a, "yh", SWAP)
    over_core = lambda a: lax.ppermute(a, "core", SWAP)
    def after(block, state):
        return lax.optimization_barrier((block, state))

    own_kv, own_q, other = pack(q, k, v, qt, kt, vt)
    peer = over_y(other)
    core_kv = over_core(own_kv)
    near = [hop(own_kv), hop(core_kv)]
    near_next = [hop(a) for a in near]
    core_q = over_core(own_q)
    first, peer, core_q = lax.optimization_barrier((near_next[0], peer, core_q))
    peer_core = over_core(peer)
    second, peer_kv = after(near_next[1], peer[:tokens])
    near_three = [hop(first), hop(second)]
    far = [hop(peer_kv), hop(peer_core[:tokens])]
    state, query = begin(own_kv, own_q, core_q, peer, peer_core)

    def turn(pair, state, count):
        sent, kept = [], []
        for i, block in enumerate(pair):
            block, state = after(block, state)
            kept.append(block)
            if i < count:
                sent.append(hop(block))
        return kept, sent, state

    state = attend(query, near, state)
    state = attend(query, near_next, state)
    far, far_next, state = turn(far, state, 2)
    state = attend(query, far, state)
    near, near_last, state = turn(near_three, state, 1)
    state = attend(query, near, state)
    far, far_next, state = turn(far_next, state, 2)
    state = attend(query, far, state)
    far, far_last, state = turn(far_next, state, 1)
    state = attend(query, far, state)
    last_near, state = after(near_last[0], state)
    state = attend(query, [last_near], state)
    ends = far_last
    rows = query.shape[0]
    there, there_stat = attend(query, ends, state, (rows // 2, rows), BF16)
    come, come_stat = over_core(there), over_core(there_stat)
    here, here_stat = attend(query, ends, state, (0, rows // 2), F32)
    keep, send, squares = join(here, here_stat, come, come_stat)
    come = over_y(send)
    squares = lax.all_to_all(squares, ("yh", "yl", "x"), 0, 0, tiled=True)
    return finish(keep, come, squares)


def solution(mesh):
    fine = Mesh(mesh.devices.reshape(2, -1, 2, 2, mesh.shape["head"] // 2), ("yh", "z", "core", "yl", "x"))
    spec = P(("yh", "z", "core"), ("yl", "x"))
    return jax.shard_map(
        functools.partial(on_device, fine.shape["z"]),
        mesh=fine,
        in_specs=(spec,) * 6,
        out_specs=(spec, spec),
        check_vma=False,
    )
```
